32 devices in a mesh: req: 8 (over z, x), head: 4 (over y, core).
Axes of the slice: x: 2, y: 2, z: 4, core: 2. Of those that a mesh axis runs over, the one named last changes fastest.
Arguments:
- hidden: bfloat16 [192, 1280], P('req'), may hold values from -6 to 6
- w_qkv: bfloat16 [3, 1280, 1280], P(None, None, 'head'), may hold values from -0.15625 to 0.15625
- w_out: bfloat16 [1280, 1280], P('head'), may hold values from -0.15625 to 0.15625
- s_qk: float32 [1280], P('head'), may hold values from 0.5 to 2
- alpha_attn: float32 [1280], replicated, may hold values from 0.05 to 0.5
- w_gate_up: bfloat16 [2, 1280, 2560], P(None, None, 'head'), may hold values from -0.15625 to 0.15625
- w_down: bfloat16 [2560, 1280], P('head'), may hold values from -0.125 to 0.125
- s_up: float32 [2560], P('head'), may hold values from 0.5 to 2
- s_gate: float32 [2560], P('head'), may hold values from 0.5 to 2
- alpha_mlp: float32 [1280], replicated, may hold values from 0.05 to 0.5
- short_keys: bfloat16 [192, 128, 1280], P('req', None, 'head')
- short_values: bfloat16 [192, 128, 1280], P('req', None, 'head'), may hold values from -6 to 6
- cache_lengths: int32 [192], P('req'), may hold values from 1 to 128, as said below
- long_keys: bfloat16 [4, 2048, 1280], P(None, 'req', 'head')
- long_values: bfloat16 [4, 2048, 1280], P(None, 'req', 'head'), may hold values from -6 to 6
- long_rows: int32 [4], replicated, may hold values from 0 to 191, as said below
Outputs:
- updated: bfloat16 [192, 1280], P('req')
The draws below stay inside these ranges and needn't reach their ends.
Inputs may be any that keep to these rules, and one draw needn't show every extreme that they name: `cache_lengths`: the entries of the rows named by long_rows are not read. `long_rows`: 4 distinct request rows.
All inputs are finite; a program needn't handle non-finite values.
Results may differ from the reference program's by a relative error of at most 0.011.
Values may be sent and summed in bfloat16 or wider, within the bound.
No kernel may reach another device: no remote copies, remote signals or barrier semaphores. Data moves between devices by JAX's collectives and lax.ppermute only.
A program may use at most 64 MiB of HBM per device.

```python
import math
import jax
import jax.numpy as jnp
from jax import lax

D = 1280
HEADS = 20
HEAD_DIM = 64
FF = 2560
SHORT = 128
LONGS = 4
REQ_DEV = 24
LONG_DEV = 256
REQS = 192
LONG = 2048


def pick_long_rows(key):
    inner = jax.random.permutation(jax.random.fold_in(key, 11), REQS - 2)[:LONGS - 2].astype(jnp.int32) + 1
    ends = jnp.array([0, REQS - 1], dtype=jnp.int32)
    chosen = jnp.concatenate([ends, inner])
    order = jax.random.permutation(jax.random.fold_in(key, 13), LONGS)
    return chosen[order].astype(jnp.int32)


def draw_short_keys(key, part):
    shape = (REQS, SHORT, D)
    base = jax.random.normal(jax.random.fold_in(key, 1), shape, jnp.float32) * 0.125
    return base.astype(jnp.bfloat16)


def draw_long_keys(key, part):
    blocks = LONG // LONG_DEV
    chosen = pick_long_rows(key)
    owner = chosen // REQ_DEV
    offset = jax.random.randint(jax.random.fold_in(key, 3), (LONGS,), 1, blocks, dtype=jnp.int32)
    strongest = (owner + offset) % blocks
    low_level = 0.0
    base = jax.random.normal(jax.random.fold_in(key, 1), (LONGS, blocks, LONG_DEV, D), jnp.float32) * 0.125
    levels = jnp.exp(jax.random.uniform(jax.random.fold_in(key, 5), (LONGS, blocks), jnp.float32, low_level, math.log(100.0)))
    block_ids = jnp.arange(blocks, dtype=jnp.int32)[None, :]
    levels = jnp.where(block_ids == strongest[:, None], 100.0, levels)
    quiet = jnp.exp(jax.random.uniform(jax.random.fold_in(key, 9), (LONGS, blocks), jnp.float32, math.log(0.5), 0.0))
    levels = jnp.where(block_ids == owner[:, None], quiet, levels)
    keys = base * levels[:, :, None, None]
    return keys.reshape(LONGS, LONG, D).astype(jnp.bfloat16)


def draw_cache_lengths(key, part):
    values = jax.random.randint(key, (REQS,), 1, SHORT + 1, dtype=jnp.int32)
    where = jax.random.randint(jax.random.fold_in(key, 3), (), 0, REQS, dtype=jnp.int32)
    return values.at[where].set(SHORT)


def draw_long_rows(key, part):
    return pick_long_rows(key)


def block_scale(own_key, shape, pieces, least, largest):
    def one(axis_at, parts):
        heights = jax.random.uniform(jax.random.fold_in(jax.random.fold_in(own_key, 6), axis_at), (parts,), jnp.float32, least / len(pieces), largest / len(pieces))
        return jnp.repeat(jnp.exp(heights), shape[axis_at] // parts).reshape((-1,) + (1,) * (len(shape) - axis_at - 1))

    factor_of = one(*pieces[0])
    for cut in pieces[1:]:
        factor_of = factor_of * one(*cut)
    return factor_of


def noise(stream_key, dims, scale, reach, pieces=(), kind=jnp.bfloat16):
    values = scale * jax.random.normal(stream_key, dims, jnp.float32)
    if pieces:
        values = values * block_scale(stream_key, dims, pieces, -0.22, 0.18)
    return jnp.clip(values, -reach, reach).astype(kind)


def setup_inputs(seed: int = 0) -> dict:
    key_of = jax.random.split(jax.random.key(seed), 17)
    return {
        "hidden": noise(key_of[0], (REQS, D), 1.0, 6.0, ((0, 8),)),
        "w_qkv": noise(key_of[1], (3, D, D), D ** -0.5, 0.15625, ((2, 4),)),
        "w_out": noise(key_of[2], (D, D), D ** -0.5, 0.15625, ((0, 4),)),
        "s_qk": jnp.clip(jnp.exp(math.log(2.0) - 1.3862944 * jax.random.uniform(key_of[3], (D,), jnp.float32) ** block_scale(key_of[3], (D,), ((0, 4),), -0.2, 0.2)), 0.5, 2.0),
        "alpha_attn": jnp.clip(jnp.exp(jax.random.uniform(key_of[4], (D,), jnp.float32, math.log(0.05), math.log(0.5))), 0.05, 0.5),
        "w_gate_up": noise(key_of[5], (2, D, FF), D ** -0.5, 0.15625, ((2, 4),)),
        "w_down": noise(key_of[6], (FF, D), FF ** -0.5, 0.125, ((0, 4),)),
        "s_up": jnp.clip(jnp.exp(math.log(2.0) - 1.3862944 * jax.random.uniform(key_of[7], (FF,), jnp.float32) ** block_scale(key_of[7], (FF,), ((0, 4),), -0.2, 0.2)), 0.5, 2.0),
        "s_gate": jnp.clip(jnp.exp(math.log(2.0) - 1.3862944 * jax.random.uniform(key_of[8], (FF,), jnp.float32) ** block_scale(key_of[8], (FF,), ((0, 4),), -0.2, 0.2)), 0.5, 2.0),
        "alpha_mlp": jnp.clip(jnp.exp(jax.random.uniform(key_of[9], (D,), jnp.float32, math.log(0.05), math.log(0.5))), 0.05, 0.5),
        "short_keys": draw_short_keys(jax.random.fold_in(key_of[16], 71), 0),
        "short_values": noise(key_of[11], (REQS, SHORT, D), 1.0, 6.0, ((0, 8), (2, 4))),
        "cache_lengths": draw_cache_lengths(jax.random.fold_in(key_of[16], 71), 0),
        "long_keys": draw_long_keys(jax.random.fold_in(key_of[16], 71), 0),
        "long_values": noise(key_of[14], (LONGS, LONG, D), 1.0, 6.0, ((1, 8), (2, 4))),
        "long_rows": draw_long_rows(jax.random.fold_in(key_of[16], 71), 0),
    }


EPS = 1e-06

def row_norm(values):
    return values * lax.rsqrt(lax.optimization_barrier(jnp.mean(values * values, axis=-1, keepdims=True)) + EPS)

def head_unit(values, gains):
    shaped = values.reshape(values.shape[:-1] + (HEADS, HEAD_DIM))
    scaled = shaped * lax.rsqrt(lax.optimization_barrier(jnp.sum(shaped * shaped, axis=-1, keepdims=True)) + EPS)
    return scaled.reshape(values.shape) * gains

def attend_one(query, key_new, value_new, keys, values, valid):
    query32 = query.astype(jnp.float32)
    scale = math.sqrt(HEAD_DIM)
    scores = scale * jnp.einsum('hd,jhd->hj', query32, keys.astype(jnp.float32))
    scores = jnp.where(valid[None, :], scores, -1e+30)
    own = scale * lax.optimization_barrier(jnp.sum(query32 * key_new.astype(jnp.float32), axis=-1))
    top = jnp.maximum(lax.optimization_barrier(jnp.max(scores, axis=-1)), own)
    weights = jnp.where(valid[None, :], jnp.exp(scores - top[:, None]), 0.0)
    own_weight = jnp.exp(own - top)
    total = lax.optimization_barrier(jnp.sum(weights, axis=-1)) + own_weight
    summed = jnp.einsum('hj,jhd->hd', weights.astype(jnp.bfloat16).astype(jnp.float32), values.astype(jnp.float32))
    summed = summed + own_weight.astype(jnp.bfloat16).astype(jnp.float32)[:, None] * value_new.astype(jnp.float32)
    return summed / total[:, None]

def reference(hidden, w_qkv, w_out, s_qk, alpha_attn, w_gate_up, w_down, s_up, s_gate, alpha_mlp, short_keys, short_values, cache_lengths, long_keys, long_values, long_rows):
    query = jnp.dot(hidden, w_qkv[0], preferred_element_type=jnp.float32)
    key_new = jnp.dot(hidden, w_qkv[1], preferred_element_type=jnp.float32)
    value_new = jnp.dot(hidden, w_qkv[2], preferred_element_type=jnp.float32)
    query_unit = head_unit(query, s_qk).astype(jnp.bfloat16).reshape(REQS, HEADS, HEAD_DIM)
    key_unit = head_unit(key_new, s_qk).astype(jnp.bfloat16).reshape(REQS, HEADS, HEAD_DIM)
    value_heads = value_new.astype(jnp.bfloat16).reshape(REQS, HEADS, HEAD_DIM)
    blocks = REQS // 8
    valid = jnp.arange(SHORT, dtype=jnp.int32)[None, :] < cache_lengths[:, None]

    def block_fn(packed):
        return jax.vmap(attend_one)(*packed)
    packed = (query_unit.reshape(blocks, 8, HEADS, HEAD_DIM), key_unit.reshape(blocks, 8, HEADS, HEAD_DIM), value_heads.reshape(blocks, 8, HEADS, HEAD_DIM), short_keys.reshape(blocks, 8, SHORT, HEADS, HEAD_DIM), short_values.reshape(blocks, 8, SHORT, HEADS, HEAD_DIM), valid.reshape(blocks, 8, SHORT))
    attended = lax.map(block_fn, packed).reshape(REQS, HEADS, HEAD_DIM)
    always = jnp.ones((LONG,), dtype=bool)
    for index in range(LONGS):
        row = long_rows[index]
        result = attend_one(query_unit[row], key_unit[row], value_heads[row], long_keys[index].reshape(LONG, HEADS, HEAD_DIM), long_values[index].reshape(LONG, HEADS, HEAD_DIM), always)
        attended = attended.at[row].set(result)
    attended = attended.astype(jnp.bfloat16).reshape(REQS, D)
    base = hidden.astype(jnp.float32)
    projected = jnp.dot(attended, w_out, preferred_element_type=jnp.float32)
    middle = row_norm(base + alpha_attn * (row_norm(projected) - base)).astype(jnp.bfloat16)
    gate = jnp.dot(middle, w_gate_up[0], preferred_element_type=jnp.float32) * s_gate
    upward = jnp.dot(middle, w_gate_up[1], preferred_element_type=jnp.float32) * s_up
    gated = (jax.nn.silu(gate) * upward).astype(jnp.bfloat16)
    downward = jnp.dot(gated, w_down, preferred_element_type=jnp.float32)
    middle32 = middle.astype(jnp.float32)
    return row_norm(middle32 + alpha_mlp * (row_norm(downward) - middle32)).astype(jnp.bfloat16)
```

```python
import functools
import math

import jax
import jax.numpy as jnp
from jax import lax
from jax.experimental import pallas as pl
from jax.experimental.pallas import tpu as pltpu
from jax.sharding import PartitionSpec as P

HEAD_DIM = 64
EPS = 1e-06
LOW = -1e30
F32 = jnp.float32
BF16 = jnp.bfloat16

VMEM = pl.BlockSpec(memory_space=pltpu.VMEM)
SMEM = pl.BlockSpec(memory_space=pltpu.SMEM)


def head_masks(width):
    lane = lax.broadcasted_iota(jnp.int32, (1, width), 1)
    return [
        (lane >= h * HEAD_DIM) & (lane < (h + 1) * HEAD_DIM) for h in range(width // HEAD_DIM)
    ]


def spread(columns, masks):
    total = jnp.where(masks[0], columns[0], 0.0)
    for mask, column in zip(masks[1:], columns[1:]):
        total = jnp.where(mask, column, total)
    return total


def head_sums(values, masks):
    return [jnp.sum(jnp.where(mask, values, 0.0), axis=-1, keepdims=True) for mask in masks]


def head_unit(values, gains, masks):
    scales = [lax.rsqrt(s + EPS) for s in head_sums(values * values, masks)]
    return (values * spread(scales, masks) * gains).astype(BF16).astype(F32)


def row_norm(values):
    return values * lax.rsqrt(jnp.mean(values * values, axis=-1, keepdims=True) + EPS)


def by_head(values, masks):
    return jnp.concatenate([jnp.where(mask, values, 0.0) for mask in masks], axis=0)


def attend(query, keys, values, valid, own, own_value, masks):
    rows = query.shape[0]
    scores = lax.dot_general(
        by_head(query, masks).astype(BF16),
        keys,
        (((1,), (1,)), ((), ())),
        preferred_element_type=F32,
    )
    tops, totals, fresh, weights = [], [], [], []
    for h in range(len(masks)):
        part = jnp.where(valid, scores[h * rows : (h + 1) * rows], LOW)
        top = jnp.max(part, axis=-1, keepdims=True)
        if own is not None:
            top = jnp.maximum(top, own[h])
        weight = jnp.where(valid, jnp.exp(part - top), 0.0)
        total = jnp.sum(weight, axis=-1, keepdims=True)
        if own is not None:
            fresh.append(jnp.exp(own[h] - top))
            total = total + fresh[-1]
        tops.append(top)
        totals.append(total)
        weights.append(weight)
    summed = jnp.dot(
        jnp.concatenate(weights, axis=0).astype(BF16), values, preferred_element_type=F32
    )
    acc = jnp.zeros(query.shape, F32)
    for h, mask in enumerate(masks):
        acc = jnp.where(mask, summed[h * rows : (h + 1) * rows], acc)
    if own is not None:
        acc = acc + spread(fresh, masks).astype(BF16).astype(F32) * own_value
    total = spread(totals, masks)
    return acc / total, spread(tops, masks) + jnp.log(total)


def short_kernel(
    lengths_ref, local_ref, hidden_ref, w_ref, gains_ref, keys_ref, values_ref, out_ref, lse_ref
):
    rows, width = out_ref.shape
    slots = keys_ref.shape[0] // rows
    masks = head_masks(width)
    hidden = hidden_ref[...]
    gains = gains_ref[...]
    query = jnp.dot(hidden, w_ref[0], preferred_element_type=F32)
    key_new = jnp.dot(hidden, w_ref[1], preferred_element_type=F32)
    value_new = jnp.dot(hidden, w_ref[2], preferred_element_type=F32).astype(BF16).astype(F32)
    query = head_unit(query, gains, masks) * math.sqrt(HEAD_DIM)
    key_new = head_unit(key_new, gains, masks)
    own = head_sums(query * key_new, masks)
    group = 8
    sub = lax.broadcasted_iota(jnp.int32, (group, slots), 0)
    lane = lax.broadcasted_iota(jnp.int32, (group, slots), 1)
    for start in range(0, rows, group):
        pieces = []
        for r in range(group):
            length = lengths_ref[start + r]
            for index in range(local_ref.shape[0]):
                length = jnp.where(local_ref[index] == start + r, 0, length)
            pieces.append((sub == r) & (lane < length))
        valid = jnp.concatenate([p.astype(F32) for p in pieces], axis=1) > 0.5
        span = slice(start, start + group)
        cached = slice(start * slots, (start + group) * slots)
        out, lse = attend(
            query[span],
            keys_ref[cached, :],
            values_ref[cached, :],
            valid,
            [o[span] for o in own],
            value_new[span],
            masks,
        )
        out_ref[span, :] = out
        lse_ref[span, :] = lse


def long_kernel(hidden_ref, w_ref, gains_ref, keys_ref, values_ref, sent_ref):
    longs = hidden_ref.shape[0]
    parties, rows, width = sent_ref.shape
    span = keys_ref.shape[0] // longs
    masks = head_masks(width)
    query = jnp.dot(hidden_ref[...], w_ref[0], preferred_element_type=F32)
    query = jnp.concatenate([query, jnp.zeros((rows - longs, width), F32)], axis=0)
    query = head_unit(query, gains_ref[...], masks) * math.sqrt(HEAD_DIM)
    sub = lax.broadcasted_iota(jnp.int32, (rows, span * longs), 0)
    lane = lax.broadcasted_iota(jnp.int32, (rows, span * longs), 1)
    valid = (lane >= sub * span) & (lane < (sub + 1) * span)
    valid = valid | ((sub >= longs) & (lane < span))
    out, lse = attend(query, keys_ref[...], values_ref[...], valid, None, None, masks)
    packed = jnp.concatenate([out[:longs], lse[:longs]], axis=0)
    for party in range(parties):
        sent_ref[party] = packed


def project_kernel(local_ref, parts_ref, short_ref, lse_ref, w_ref, out_ref):
    parties, doubled, width = parts_ref.shape
    longs = doubled // 2
    rows = short_ref.shape[0]
    top = parts_ref[0]
    for party in range(1, parties):
        top = jnp.maximum(top, parts_ref[party])
    top = top[longs:]
    total = jnp.zeros((longs, width), F32)
    acc = jnp.zeros((longs, width), F32)
    for party in range(parties):
        part = parts_ref[party]
        weight = jnp.exp(part[longs:] - top)
        total = total + weight
        acc = acc + weight * part[:longs]
    long_out = acc / total
    long_lse = top + jnp.log(total)
    row = lax.broadcasted_iota(jnp.int32, (rows, 1), 0)
    placed = jnp.zeros((rows, width), F32)
    placed_lse = jnp.full((rows, width), LOW, F32)
    for index in range(longs):
        here = row == local_ref[index]
        placed = jnp.where(here, long_out[index : index + 1], placed)
        placed_lse = jnp.where(here, long_lse[index : index + 1], placed_lse)
    short_lse = lse_ref[...]
    top = jnp.maximum(short_lse, placed_lse)
    near = jnp.exp(short_lse - top)
    far = jnp.exp(placed_lse - top)
    attended = (near * short_ref[...] + far * placed) / (near + far)
    out_ref[...] = jnp.dot(
        attended.astype(BF16), w_ref[...], preferred_element_type=F32
    ).astype(BF16)


def renormed(parts_ref, base, alpha):
    total = parts_ref[0].astype(F32)
    for part in range(1, parts_ref.shape[0]):
        total = total + parts_ref[part].astype(F32)
    return row_norm(base + alpha * (row_norm(total) - base)).astype(BF16)


def mlp_kernel(
    parts_ref, hidden_ref, alpha_ref, w_gate_up_ref, gate_ref, up_ref, w_down_ref, mid_ref, out_ref
):
    middle = renormed(parts_ref, hidden_ref[...].astype(F32), alpha_ref[...])
    mid_ref[...] = middle
    gate = jnp.dot(middle, w_gate_up_ref[0], preferred_element_type=F32) * gate_ref[...]
    upward = jnp.dot(middle, w_gate_up_ref[1], preferred_element_type=F32) * up_ref[...]
    gated = (gate / (1.0 + jnp.exp(-gate)) * upward).astype(BF16)
    out_ref[...] = jnp.dot(gated, w_down_ref[...], preferred_element_type=F32).astype(BF16)


def final_kernel(parts_ref, mid_ref, alpha_ref, out_ref):
    out_ref[...] = renormed(parts_ref, mid_ref[...].astype(F32), alpha_ref[...])


def call(kernel, specs, out_shape, cost, *operands):
    return pl.pallas_call(
        kernel,
        in_specs=specs,
        out_specs=jax.tree.map(lambda _: VMEM, out_shape),
        out_shape=out_shape,
        cost_estimate=pl.CostEstimate(flops=cost[0], bytes_accessed=cost[1], transcendentals=0),
        compiler_params=pltpu.CompilerParams(vmem_limit_bytes=24 * 1024 * 1024),
    )(*operands)


def on_device(
    hidden,
    w_qkv,
    w_out,
    s_qk,
    alpha_attn,
    w_gate_up,
    w_down,
    s_up,
    s_gate,
    alpha_mlp,
    short_keys,
    short_values,
    cache_lengths,
    long_keys,
    long_values,
    long_rows,
):
    rows, model = hidden.shape
    width = w_qkv.shape[2]
    longs, span = long_keys.shape[:2]
    slots = short_keys.shape[1]
    parties = lax.axis_size("req")
    local = long_rows - lax.axis_index("req") * rows
    with jax.named_scope("long_hidden"):
        matches = (local[:, None] == jnp.arange(rows, dtype=jnp.int32)[None, :]).astype(BF16)
        picked = jnp.dot(matches, hidden, preferred_element_type=F32).astype(BF16)
        sent = jnp.broadcast_to(picked[None], (parties, longs, model))
        long_hidden = jnp.sum(lax.all_to_all(sent, "req", 0, 0), axis=0, dtype=F32).astype(BF16)
    gains = s_qk[None, :]
    with jax.named_scope("short_attention"):
        short_out, short_lse = call(
            short_kernel,
            [SMEM, SMEM] + [VMEM] * 5,
            (jax.ShapeDtypeStruct((rows, width), F32),) * 2,
            (10**9, 64 * 10**5),
            cache_lengths,
            local,
            hidden,
            w_qkv,
            gains,
            short_keys.reshape(rows * slots, width),
            short_values.reshape(rows * slots, width),
        )
    with jax.named_scope("long_attention"):
        partial = call(
            long_kernel,
            [VMEM] * 5,
            jax.ShapeDtypeStruct((parties, 2 * longs, width), F32),
            (10**8, 2 * 10**6),
            long_hidden,
            w_qkv,
            gains,
            long_keys.reshape(longs * span, width),
            long_values.reshape(longs * span, width),
        )
    with jax.named_scope("long_parts"):
        parts = lax.all_to_all(partial, "req", 0, 0)
    with jax.named_scope("project"):
        projected = call(
            project_kernel,
            [SMEM] + [VMEM] * 4,
            jax.ShapeDtypeStruct((rows, model), BF16),
            (2 * rows * width * model, 10**6),
            local,
            parts,
            short_out,
            short_lse,
            w_out,
        )
    with jax.named_scope("sum_heads"):
        projected = lax.all_gather(projected, "head")
    with jax.named_scope("mlp"):
        middle, downward = call(
            mlp_kernel,
            [VMEM] * 7,
            (jax.ShapeDtypeStruct((rows, model), BF16),) * 2,
            (10**8, 5 * 10**6),
            projected,
            hidden,
            alpha_attn[None, :],
            w_gate_up,
            s_gate[None, :],
            s_up[None, :],
            w_down,
        )
    with jax.named_scope("sum_units"):
        downward = lax.all_gather(downward, "head")
    with jax.named_scope("final"):
        return call(
            final_kernel,
            [VMEM] * 3,
            jax.ShapeDtypeStruct((rows, model), BF16),
            (10**6, 10**5),
            downward,
            middle,
            alpha_mlp[None, :],
        )


def solution(mesh):
    return jax.shard_map(
        on_device,
        mesh=mesh,
        in_specs=(
            P("req", None),
            P(None, None, "head"),
            P("head", None),
            P("head"),
            P(),
            P(None, None, "head"),
            P("head", None),
            P("head"),
            P("head"),
            P(),
            P("req", None, "head"),
            P("req", None, "head"),
            P("req"),
            P(None, "req", "head"),
            P(None, "req", "head"),
            P(),
        ),
        out_specs=P("req", None),
        check_vma=False,
    )
```

```python
import math

import jax
import jax.numpy as jnp
from jax import lax
from jax.experimental import pallas as pl
from jax.experimental.pallas import tpu as pltpu
from jax.sharding import PartitionSpec as P

HEAD_DIM = 64
EPS = 1e-06
LOW = -1e30
F32 = jnp.float32
BF16 = jnp.bfloat16
LANES = 8

VMEM = pl.BlockSpec(memory_space=pltpu.VMEM)
HBM = pl.BlockSpec(memory_space=pltpu.HBM)


def dot(left, right):
    return jnp.dot(left, right, preferred_element_type=F32)


def dot_t(left, right):
    return lax.dot_general(left, right, (((1,), (1,)), ((), ())), preferred_element_type=F32)


def head_masks(width):
    lane = lax.broadcasted_iota(jnp.int32, (1, width), 1)
    return [
        (lane >= h * HEAD_DIM) & (lane < (h + 1) * HEAD_DIM) for h in range(width // HEAD_DIM)
    ]


def head_rows(width):
    sub = lax.broadcasted_iota(jnp.int32, (LANES, width), 0)
    lane = lax.broadcasted_iota(jnp.int32, (LANES, width), 1)
    return (lane >= sub * HEAD_DIM) & (lane < (sub + 1) * HEAD_DIM)


def head_unit(values, gains, masks):
    squares = values * values
    scale = jnp.zeros_like(values)
    for mask in masks:
        total = jnp.sum(jnp.where(mask, squares, 0.0), axis=-1, keepdims=True)
        scale = jnp.where(mask, lax.rsqrt(total + EPS), scale)
    return (values * scale * gains).astype(BF16).astype(F32)


def row_norm(values):
    return values * lax.rsqrt(jnp.mean(values * values, axis=-1, keepdims=True) + EPS)


def gathered(values, diagonal):
    return jnp.sum(jnp.where(diagonal, values, 0.0), axis=0, keepdims=True)


def start_all(pairs, sems):
    copies = [pltpu.make_async_copy(s, d, sems.at[i]) for i, (s, d) in enumerate(pairs)]
    for copy in copies:
        copy.start()
    return copies


def select_kernel(
    longs_hbm,
    hidden_hbm,
    w_hbm,
    keys_hbm,
    values_hbm,
    sent_hbm,
    hidden_ref,
    w_query_ref,
    keys_ref,
    values_ref,
    longs_ref,
    sent_ref,
    sems,
):
    copies = start_all(
        [
            (longs_hbm, longs_ref),
            (hidden_hbm, hidden_ref),
            (w_hbm.at[0], w_query_ref),
            (keys_hbm, keys_ref),
            (values_hbm, values_ref),
        ],
        sems,
    )
    parties, longs, _ = sent_ref.shape
    rows = hidden_ref.shape[0]
    offset = lax.axis_index("req") * rows
    sub = lax.broadcasted_iota(jnp.int32, (8, rows), 0)
    lane = lax.broadcasted_iota(jnp.int32, (8, rows), 1) + offset
    here = jnp.zeros((8, rows), jnp.bool_)
    copies[0].wait()
    for index in range(longs):
        here = here | ((sub == index) & (lane == longs_ref[index]))
    copies[1].wait()
    picked = dot(here.astype(F32).astype(BF16), hidden_ref[...])[:longs].astype(BF16)
    for party in range(parties):
        sent_ref[party] = picked
    out = pltpu.make_async_copy(sent_ref, sent_hbm, sems.at[5])
    out.start()
    out.wait()
    for copy in copies[2:]:
        copy.wait()


def qkv_kernel(
    gains_hbm,
    w_hbm,
    hidden_ref,
    w_query_ref,
    query_ref,
    key_ref,
    value_ref,
    gains_ref,
    w_key_ref,
    w_value_ref,
    sems,
):
    copies = start_all(
        [(gains_hbm, gains_ref), (w_hbm.at[1], w_key_ref), (w_hbm.at[2], w_value_ref)], sems
    )
    masks = head_masks(query_ref.shape[1])
    hidden = hidden_ref[...]
    query = dot_t(hidden, w_query_ref[...])
    copies[0].wait()
    gains = gains_ref[...][None, :]
    query_ref[...] = head_unit(query, gains, masks) * math.sqrt(HEAD_DIM)
    copies[1].wait()
    key_ref[...] = head_unit(dot_t(hidden, w_key_ref[...]), gains, masks)
    copies[2].wait()
    value_ref[...] = dot_t(hidden, w_value_ref[...]).astype(BF16).astype(F32)


def long_kernel(
    received_ref,
    gains_ref,
    w_ref,
    keys_ref,
    values_ref,
    sent_hbm,
    sent_ref,
    sems,
):
    parties, longs, _ = received_ref.shape
    width = w_ref.shape[0]
    hidden = received_ref[0].astype(F32)
    for party in range(1, parties):
        hidden = hidden + received_ref[party].astype(F32)
    query = dot_t(hidden.astype(BF16), w_ref[...])
    query = head_unit(query, gains_ref[...][None, :], head_masks(width)) * math.sqrt(HEAD_DIM)
    diagonal = head_rows(width)
    scores = [
        dot(jnp.where(diagonal, query[i : i + 1], 0.0).astype(BF16), keys_ref[i])
        for i in range(longs)
    ]
    outs, lses = [], []
    for i in range(longs):
        top = jnp.max(scores[i], axis=-1, keepdims=True)
        weights = jnp.exp(scores[i] - top)
        total = jnp.sum(weights, axis=-1, keepdims=True)
        summed = dot_t(weights.astype(BF16), values_ref[i])
        outs.append(gathered(summed / total, diagonal))
        lses.append(gathered(top + jnp.log(total), diagonal))
    packed = jnp.concatenate(outs + lses, axis=0)
    for party in range(parties):
        sent_ref[party] = packed
    out = pltpu.make_async_copy(sent_ref, sent_hbm, sems.at[0])
    out.start()
    out.wait()


def short_kernel(
    lengths_hbm,
    longs_hbm,
    keys_hbm,
    values_hbm,
    w_out_hbm,
    query_ref,
    key_ref,
    value_ref,
    out_ref,
    lse_ref,
    match_ref,
    w_out_ref,
    lengths_ref,
    longs_ref,
    keys_ref,
    values_ref,
    sems,
):
    rows, width = out_ref.shape
    slots = keys_ref.shape[2]
    longs = longs_ref.shape[0]
    group = 8
    parts = [pl.ds(start, group) for start in range(0, rows, group)]
    copies = start_all(
        [(lengths_hbm, lengths_ref), (longs_hbm, longs_ref)]
        + [(keys_hbm.at[part], keys_ref.at[part]) for part in parts]
        + [(values_hbm.at[part], values_ref.at[part]) for part in parts]
        + [(w_out_hbm, w_out_ref)],
        sems,
    )
    key_copies = copies[2 : 2 + len(parts)]
    value_copies = copies[2 + len(parts) : -1]
    offset = lax.axis_index("req") * rows
    diagonal = head_rows(width)
    sub = lax.broadcasted_iota(jnp.int32, (2 * LANES, 2 * slots), 0)
    lane = lax.broadcasted_iota(jnp.int32, (2 * LANES, 2 * slots), 1)
    second = sub >= LANES
    first = jnp.where(second, slots, 0)
    query = query_ref[...]
    key = key_ref[...]
    value = value_ref[...]
    pairs, owns = [], []
    for r in range(0, rows, 2):
        pair = jnp.concatenate(
            [jnp.where(diagonal, query[r + i : r + i + 1], 0.0) for i in range(2)], axis=0
        )
        new = jnp.concatenate(
            [jnp.where(diagonal, key[r + i : r + i + 1], 0.0) for i in range(2)], axis=0
        )
        owns.append(jnp.sum(pair * new, axis=-1, keepdims=True))
        pairs.append(pair.astype(BF16))
    copies[0].wait()
    copies[1].wait()
    row = lax.broadcasted_iota(jnp.int32, match_ref.shape, 0) + offset
    column = lax.broadcasted_iota(jnp.int32, match_ref.shape, 1)
    match = jnp.zeros(match_ref.shape, F32)
    for index in range(longs):
        match = jnp.where((row == longs_ref[index]) & (column == index), 1.0, match)
    match_ref[...] = match
    weights, scales, fresh = [], [], []
    for p, r in enumerate(range(0, rows, 2)):
        if r % group == 0:
            key_copies[r // group].wait()
        scores = dot(pairs[p], jnp.concatenate([keys_ref[r], keys_ref[r + 1]], axis=1))
        lengths = []
        for i in range(2):
            length = lengths_ref[r + i]
            for index in range(longs):
                length = jnp.where(longs_ref[index] == offset + r + i, 0, length)
            lengths.append(length)
        valid = (lane >= first) & (lane < jnp.where(second, slots + lengths[1], lengths[0]))
        scores = jnp.where(valid, scores, LOW)
        top = jnp.maximum(jnp.max(scores, axis=-1, keepdims=True), owns[p])
        weight = jnp.where(valid, jnp.exp(scores - top), 0.0)
        own = jnp.exp(owns[p] - top)
        total = jnp.sum(weight, axis=-1, keepdims=True) + own
        weights.append(weight.astype(BF16))
        scales.append(total)
        fresh.append(own.astype(BF16).astype(F32))
        lse = top + jnp.log(total)
        for i in range(2):
            part = slice(i * LANES, (i + 1) * LANES)
            lse_ref[r + i : r + i + 1, :] = gathered(lse[part], diagonal)
    for p, r in enumerate(range(0, rows, 2)):
        if r % group == 0:
            value_copies[r // group].wait()
        summed = dot_t(
            weights[p], jnp.concatenate([values_ref[r], values_ref[r + 1]], axis=1)
        )
        for i in range(2):
            part = slice(i * LANES, (i + 1) * LANES)
            acc = summed[part] + fresh[p][part] * value[r + i : r + i + 1]
            out_ref[r + i : r + i + 1, :] = gathered(acc / scales[p][part], diagonal)
    copies[-1].wait()


def project_kernel(parts_ref, short_ref, lse_ref, match_ref, w_ref, out_ref):
    parties, doubled, width = parts_ref.shape
    longs = doubled // 2
    rows = short_ref.shape[0]
    top = parts_ref[0]
    for party in range(1, parties):
        top = jnp.maximum(top, parts_ref[party])
    top = top[longs:]
    total = jnp.zeros((longs, width), F32)
    acc = jnp.zeros((longs, width), F32)
    for party in range(parties):
        part = parts_ref[party]
        weight = jnp.exp(part[longs:] - top)
        total = total + weight
        acc = acc + weight * part[:longs]
    long_out = acc / total
    long_lse = top + jnp.log(total)
    placed = jnp.zeros((rows, width), F32)
    placed_lse = jnp.full((rows, width), LOW, F32)
    for index in range(longs):
        here = match_ref[:, index : index + 1] > 0.5
        placed = jnp.where(here, long_out[index : index + 1], placed)
        placed_lse = jnp.where(here, long_lse[index : index + 1], placed_lse)
    short_lse = lse_ref[...]
    top = jnp.maximum(short_lse, placed_lse)
    near = jnp.exp(short_lse - top)
    far = jnp.exp(placed_lse - top)
    attended = (near * short_ref[...] + far * placed) / (near + far)
    out_ref[...] = dot(attended.astype(BF16), w_ref[...]).astype(BF16)


def load_kernel(*refs):
    count = (len(refs) - 2) // 2
    copies = start_all(list(zip(refs[:count], refs[count + 1 : -1])), refs[-1])
    for copy in copies:
        copy.wait()


def add_kernel(left_ref, right_ref, *refs):
    out_ref = refs[-1]
    out_ref[...] = (left_ref[...].astype(F32) + right_ref[...].astype(F32)).astype(BF16)


def renormed(left_ref, right_ref, base, alpha_ref):
    total = left_ref[...].astype(F32) + right_ref[...].astype(F32)
    alpha = alpha_ref[...][None, :]
    return row_norm(base + alpha * (row_norm(total) - base)).astype(BF16)


def mlp_kernel(
    left_ref,
    right_ref,
    hidden_ref,
    alpha_ref,
    w_gate_up_ref,
    w_down_ref,
    s_gate_ref,
    s_up_ref,
    mid_ref,
    out_ref,
):
    middle = renormed(left_ref, right_ref, hidden_ref[...].astype(F32), alpha_ref)
    mid_ref[...] = middle
    gate = dot(middle, w_gate_up_ref[0]) * s_gate_ref[...][None, :]
    upward = dot(middle, w_gate_up_ref[1]) * s_up_ref[...][None, :]
    gated = (gate / (1.0 + jnp.exp(-gate)) * upward).astype(BF16)
    out_ref[...] = dot(gated, w_down_ref[...]).astype(BF16)


def final_kernel(left_ref, right_ref, mid_ref, alpha_ref, out_ref):
    out_ref[...] = renormed(left_ref, right_ref, mid_ref[...].astype(F32), alpha_ref)


def call(kernel, outs, cost, far=(), near=(), out_far=(), scratch=(), copies=0):
    far = [pltpu.with_memory_space_constraint(a, pltpu.HBM) for a in far]
    return pl.pallas_call(
        kernel,
        in_specs=[HBM] * len(far) + [VMEM] * len(near),
        out_specs=[HBM] * len(out_far) + [VMEM] * len(outs),
        out_shape=[pltpu.HBM(a.shape, a.dtype) for a in out_far] + list(outs),
        scratch_shapes=list(scratch) + [pltpu.SemaphoreType.DMA((copies,))] * (copies > 0),
        cost_estimate=pl.CostEstimate(flops=cost[0], bytes_accessed=cost[1], transcendentals=0),
        compiler_params=pltpu.CompilerParams(vmem_limit_bytes=32 * 1024 * 1024),
    )(*far, *near)


def like(array):
    return jax.ShapeDtypeStruct(array.shape, array.dtype)


def exchanged(value, step):
    places = lax.axis_size("head")
    return lax.ppermute(value, "head", [(i, i ^ step) for i in range(places)])


def on_device(
    hidden,
    w_qkv,
    w_out,
    s_qk,
    alpha_attn,
    w_gate_up,
    w_down,
    s_up,
    s_gate,
    alpha_mlp,
    short_keys,
    short_values,
    cache_lengths,
    long_keys,
    long_values,
    long_rows,
):
    rows, model = hidden.shape
    width = w_qkv.shape[2]
    longs = long_keys.shape[0]
    parties = lax.axis_size("req")
    shape = jax.ShapeDtypeStruct
    state = shape((rows, width), F32)
    wide = shape((rows, model), BF16)
    w_qkv, short_keys, short_values, long_keys, long_values = (
        jnp.swapaxes(a, 1, 2) for a in (w_qkv, short_keys, short_values, long_keys, long_values)
    )
    with jax.named_scope("long_hidden"):
        sent, hidden_near, w_query, keys, values = call(
            select_kernel,
            (wide, shape(w_qkv.shape[1:], BF16), like(long_keys), like(long_values)),
            (10**6, 3 * 10**6),
            far=(long_rows, hidden, w_qkv, long_keys, long_values),
            out_far=(shape((parties, longs, model), BF16),),
            scratch=(pltpu.SMEM((longs,), jnp.int32), pltpu.VMEM((parties, longs, model), BF16)),
            copies=6,
        )
        received = lax.all_to_all(sent, "req", 0, 0)
    with jax.named_scope("qkv"):
        query, key, value, gains = call(
            qkv_kernel,
            (state, state, state, like(s_qk)),
            (10**8, 4 * 10**6),
            far=(s_qk, w_qkv),
            near=(hidden_near, w_query),
            scratch=(pltpu.VMEM(w_qkv.shape[1:], BF16),) * 2,
            copies=3,
        )
    with jax.named_scope("long_attention"):
        (partial,) = call(
            long_kernel,
            (),
            (10**8, 4 * 10**6),
            near=(received, gains, w_query, keys, values),
            out_far=(shape((parties, 2 * longs, width), F32),),
            scratch=(pltpu.VMEM((parties, 2 * longs, width), F32),),
            copies=1,
        )
    with jax.named_scope("long_parts"):
        parts = lax.all_to_all(partial, "req", 0, 0)
    with jax.named_scope("short_attention"):
        short_out, short_lse, match, w_out = call(
            short_kernel,
            (state, state, shape((rows, 128), F32), like(w_out)),
            (10**9, 6 * 10**6),
            far=(cache_lengths, long_rows, short_keys, short_values, w_out),
            near=(query, key, value),
            scratch=(
                pltpu.SMEM((rows,), jnp.int32),
                pltpu.SMEM((longs,), jnp.int32),
                pltpu.VMEM(short_keys.shape, BF16),
                pltpu.VMEM(short_values.shape, BF16),
            ),
            copies=3 + 2 * (rows // 8),
        )
    with jax.named_scope("project"):
        (projected,) = call(
            project_kernel,
            (wide,),
            (2 * rows * width * model, 10**6),
            near=(parts, short_out, short_lse, match, w_out),
        )
    with jax.named_scope("load"):
        loads = (hidden, alpha_attn, w_gate_up, w_down, s_gate, s_up, alpha_mlp)
        hidden, alpha_attn, w_gate_up, w_down, s_gate, s_up, alpha_mlp = call(
            load_kernel,
            [like(a) for a in loads],
            (10**6, 6 * 10**6),
            far=loads,
            near=(projected,),
            copies=len(loads),
        )
    with jax.named_scope("sum_heads"):
        other = exchanged(projected, 3)
        (projected,) = call(add_kernel, (wide,), (10**5, 10**5), near=(projected, other, s_up))
        other = exchanged(projected, 1)
    with jax.named_scope("mlp"):
        middle, downward = call(
            mlp_kernel,
            (wide, wide),
            (10**8, 5 * 10**6),
            near=(projected, other, hidden, alpha_attn, w_gate_up, w_down, s_gate, s_up),
        )
    with jax.named_scope("sum_units"):
        other = exchanged(downward, 3)
        (downward,) = call(add_kernel, (wide,), (10**5, 10**5), near=(downward, other))
        other = exchanged(downward, 1)
    with jax.named_scope("final"):
        (updated,) = call(
            final_kernel, (wide,), (10**6, 10**5), near=(downward, other, middle, alpha_mlp)
        )
        return updated


def solution(mesh):
    return jax.shard_map(
        on_device,
        mesh=mesh,
        in_specs=(
            P("req", None),
            P(None, None, "head"),
            P("head", None),
            P("head"),
            P(),
            P(None, None, "head"),
            P("head", None),
            P("head"),
            P("head"),
            P(),
            P("req", None, "head"),
            P("req", None, "head"),
            P("req"),
            P(None, "req", "head"),
            P(None, "req", "head"),
            P(),
        ),
        out_specs=P("req", None),
        check_vma=False,
    )
```

```python
import math

import jax
import jax.numpy as jnp
from jax import lax
from jax.experimental import pallas as pl
from jax.experimental.pallas import tpu as pltpu
from jax.sharding import PartitionSpec as P

HEAD_DIM = 64
EPS = 1e-06
LOW = -1e30
F32 = jnp.float32
BF16 = jnp.bfloat16
LANES = 8

VMEM = pl.BlockSpec(memory_space=pltpu.VMEM)
HBM = pl.BlockSpec(memory_space=pltpu.HBM)


def dot(left, right):
    return jnp.dot(left, right, preferred_element_type=F32)


def dot_t(left, right):
    return lax.dot_general(left, right, (((1,), (1,)), ((), ())), preferred_element_type=F32)


def head_masks(width):
    lane = lax.broadcasted_iota(jnp.int32, (1, width), 1)
    return [
        (lane >= h * HEAD_DIM) & (lane < (h + 1) * HEAD_DIM) for h in range(width // HEAD_DIM)
    ]


def head_rows(width):
    sub = lax.broadcasted_iota(jnp.int32, (LANES, width), 0)
    lane = lax.broadcasted_iota(jnp.int32, (LANES, width), 1)
    return (lane >= sub * HEAD_DIM) & (lane < (sub + 1) * HEAD_DIM)


def spread_sums(values, masks, function):
    result = jnp.zeros_like(values)
    for mask in masks:
        total = jnp.sum(jnp.where(mask, values, 0.0), axis=-1, keepdims=True)
        result = jnp.where(mask, function(total), result)
    return result


def head_unit(values, gains, masks):
    scale = spread_sums(values * values, masks, lambda total: lax.rsqrt(total + EPS))
    return (values * scale * gains).astype(BF16).astype(F32)


def row_norm(values):
    return values * lax.rsqrt(jnp.mean(values * values, axis=-1, keepdims=True) + EPS)


def gathered(values, diagonal):
    return jnp.sum(jnp.where(diagonal, values, 0.0), axis=0, keepdims=True)


def start_all(pairs, sems):
    copies = [pltpu.make_async_copy(s, d, sems.at[i]) for i, (s, d) in enumerate(pairs)]
    for copy in copies:
        copy.start()
    return copies


def select_kernel(
    longs_hbm,
    hidden_hbm,
    gains_hbm,
    w_hbm,
    keys_hbm,
    sent_hbm,
    hidden_ref,
    match_ref,
    query_ref,
    gains_ref,
    w_query_ref,
    w_key_ref,
    keys_ref,
    longs_ref,
    sent_ref,
    sems,
):
    copies = start_all(
        [
            (longs_hbm, longs_ref),
            (hidden_hbm, hidden_ref),
            (gains_hbm, gains_ref),
            (w_hbm.at[0], w_query_ref),
            (w_hbm.at[1], w_key_ref),
            (keys_hbm, keys_ref),
        ],
        sems,
    )
    parties, longs, _ = sent_ref.shape
    rows = hidden_ref.shape[0]
    offset = lax.axis_index("req") * rows
    sub = lax.broadcasted_iota(jnp.int32, (8, rows), 0)
    lane = lax.broadcasted_iota(jnp.int32, (8, rows), 1) + offset
    here = jnp.zeros((8, rows), jnp.bool_)
    copies[0].wait()
    for index in range(longs):
        here = here | ((sub == index) & (lane == longs_ref[index]))
    copies[1].wait()
    picked = dot(here.astype(F32).astype(BF16), hidden_ref[...])[:longs].astype(BF16)
    for party in range(parties):
        sent_ref[party] = picked
    out = pltpu.make_async_copy(sent_ref, sent_hbm, sems.at[6])
    out.start()
    row = lax.broadcasted_iota(jnp.int32, match_ref.shape, 0) + offset
    column = lax.broadcasted_iota(jnp.int32, match_ref.shape, 1)
    match = jnp.zeros(match_ref.shape, F32)
    for index in range(longs):
        match = jnp.where((row == longs_ref[index]) & (column == index), 1.0, match)
    match_ref[...] = match
    copies[2].wait()
    copies[3].wait()
    query = dot_t(hidden_ref[...], w_query_ref[...])
    query = head_unit(query, gains_ref[...][None, :], head_masks(query.shape[1]))
    query_ref[...] = query * math.sqrt(HEAD_DIM)
    copies[4].wait()
    copies[5].wait()
    out.wait()


def short_kernel(
    lengths_hbm,
    w_hbm,
    keys_hbm,
    values_hbm,
    long_values_hbm,
    hidden_ref,
    query_ref,
    gains_ref,
    w_key_ref,
    out_ref,
    lse_ref,
    value_ref,
    own_ref,
    long_values_ref,
    lengths_ref,
    w_value_ref,
    keys_ref,
    values_ref,
    sems,
):
    copies = start_all(
        [
            (lengths_hbm, lengths_ref),
            (w_hbm.at[2], w_value_ref),
            (keys_hbm, keys_ref),
            (values_hbm, values_ref),
            (long_values_hbm, long_values_ref),
        ],
        sems,
    )
    rows, width = out_ref.shape
    slots = keys_ref.shape[2]
    masks = head_masks(width)
    diagonal = head_rows(width)
    sub = lax.broadcasted_iota(jnp.int32, (2 * LANES, 2 * slots), 0)
    lane = lax.broadcasted_iota(jnp.int32, (2 * LANES, 2 * slots), 1)
    second = sub >= LANES
    first = jnp.where(second, slots, 0)
    hidden = hidden_ref[...]
    query = query_ref[...]
    pairs = [
        jnp.concatenate(
            [jnp.where(diagonal, query[r + i : r + i + 1], 0.0) for i in range(2)], axis=0
        ).astype(BF16)
        for r in range(0, rows, 2)
    ]
    key = head_unit(dot_t(hidden, w_key_ref[...]), gains_ref[...][None, :], masks)
    own_ref[...] = spread_sums(query * key, masks, lambda total: total)
    copies[0].wait()
    copies[1].wait()
    value_ref[...] = dot_t(hidden, w_value_ref[...]).astype(BF16).astype(F32)
    copies[2].wait()
    weights, scales = [], []
    for p, r in enumerate(range(0, rows, 2)):
        scores = dot(pairs[p], jnp.concatenate([keys_ref[r], keys_ref[r + 1]], axis=1))
        last = jnp.where(second, slots + lengths_ref[r + 1], lengths_ref[r])
        valid = (lane >= first) & (lane < last)
        scores = jnp.where(valid, scores, LOW)
        top = jnp.max(scores, axis=-1, keepdims=True)
        weight = jnp.where(valid, jnp.exp(scores - top), 0.0)
        total = jnp.sum(weight, axis=-1, keepdims=True)
        weights.append(weight.astype(BF16))
        scales.append(1.0 / total)
        lse = top + jnp.log(total)
        for i in range(2):
            part = slice(i * LANES, (i + 1) * LANES)
            lse_ref[r + i : r + i + 1, :] = gathered(lse[part], diagonal)
    copies[3].wait()
    for p, r in enumerate(range(0, rows, 2)):
        summed = dot_t(weights[p], jnp.concatenate([values_ref[r], values_ref[r + 1]], axis=1))
        summed = summed * scales[p]
        for i in range(2):
            part = slice(i * LANES, (i + 1) * LANES)
            out_ref[r + i : r + i + 1, :] = gathered(summed[part], diagonal)
    copies[4].wait()


def long_kernel(
    w_out_hbm,
    received_ref,
    gains_ref,
    w_ref,
    keys_ref,
    values_ref,
    sent_ref,
    w_out_ref,
    sems,
):
    copy = pltpu.make_async_copy(w_out_hbm, w_out_ref, sems.at[0])
    copy.start()
    parties, longs, _ = received_ref.shape
    width = w_ref.shape[0]
    hidden = received_ref[0].astype(F32)
    for party in range(1, parties):
        hidden = hidden + received_ref[party].astype(F32)
    query = dot_t(hidden.astype(BF16), w_ref[...])
    query = head_unit(query, gains_ref[...][None, :], head_masks(width)) * math.sqrt(HEAD_DIM)
    diagonal = head_rows(width)
    scores = [
        dot(jnp.where(diagonal, query[i : i + 1], 0.0).astype(BF16), keys_ref[i])
        for i in range(longs)
    ]
    outs, lses = [], []
    for i in range(longs):
        top = jnp.max(scores[i], axis=-1, keepdims=True)
        weights = jnp.exp(scores[i] - top)
        total = jnp.sum(weights, axis=-1, keepdims=True)
        summed = dot_t(weights.astype(BF16), values_ref[i])
        outs.append(gathered(summed / total, diagonal))
        lses.append(gathered(top + jnp.log(total), diagonal))
    packed = jnp.concatenate(outs + lses, axis=0)
    for party in range(parties):
        sent_ref[party] = packed
    copy.wait()


def project_kernel(
    parts_ref, short_ref, short_lse_ref, value_ref, own_ref, match_ref, w_ref, out_ref
):
    parties, doubled, width = parts_ref.shape
    longs = doubled // 2
    top = parts_ref[0]
    for party in range(1, parties):
        top = jnp.maximum(top, parts_ref[party])
    top = top[longs:]
    total = jnp.zeros((longs, width), F32)
    acc = jnp.zeros((longs, width), F32)
    for party in range(parties):
        part = parts_ref[party]
        weight = jnp.exp(part[longs:] - top)
        total = total + weight
        acc = acc + weight * part[:longs]
    long_out = acc / total
    long_lse = top + jnp.log(total)
    cached = short_ref[...]
    lse = short_lse_ref[...]
    for index in range(longs):
        here = match_ref[:, index : index + 1] > 0.5
        cached = jnp.where(here, long_out[index : index + 1], cached)
        lse = jnp.where(here, long_lse[index : index + 1], lse)
    own = own_ref[...]
    top = jnp.maximum(lse, own)
    old = jnp.exp(lse - top)
    new = jnp.exp(own - top)
    attended = (old * cached + new * value_ref[...]) / (old + new)
    out_ref[...] = dot(attended.astype(BF16), w_ref[...]).astype(BF16)


def load_kernel(*refs):
    count = (len(refs) - 2) // 2
    copies = start_all(list(zip(refs[:count], refs[count + 1 : -1])), refs[-1])
    for copy in copies:
        copy.wait()


def add_kernel(left_ref, right_ref, *refs):
    out_ref = refs[-1]
    out_ref[...] = (left_ref[...].astype(F32) + right_ref[...].astype(F32)).astype(BF16)


def renormed(left_ref, right_ref, base, alpha_ref):
    total = left_ref[...].astype(F32) + right_ref[...].astype(F32)
    alpha = alpha_ref[...][None, :]
    return row_norm(base + alpha * (row_norm(total) - base)).astype(BF16)


def mlp_kernel(
    left_ref,
    right_ref,
    hidden_ref,
    alpha_ref,
    w_gate_up_ref,
    w_down_ref,
    s_gate_ref,
    s_up_ref,
    mid_ref,
    out_ref,
):
    middle = renormed(left_ref, right_ref, hidden_ref[...].astype(F32), alpha_ref)
    mid_ref[...] = middle
    gate = dot(middle, w_gate_up_ref[0]) * s_gate_ref[...][None, :]
    upward = dot(middle, w_gate_up_ref[1]) * s_up_ref[...][None, :]
    gated = (gate / (1.0 + jnp.exp(-gate)) * upward).astype(BF16)
    out_ref[...] = dot(gated, w_down_ref[...]).astype(BF16)


def final_kernel(left_ref, right_ref, mid_ref, alpha_ref, out_ref):
    out_ref[...] = renormed(left_ref, right_ref, mid_ref[...].astype(F32), alpha_ref)


def call(kernel, outs, cost, far=(), near=(), out_far=(), scratch=(), copies=0):
    far = [pltpu.with_memory_space_constraint(a, pltpu.HBM) for a in far]
    return pl.pallas_call(
        kernel,
        in_specs=[HBM] * len(far) + [VMEM] * len(near),
        out_specs=[HBM] * len(out_far) + [VMEM] * len(outs),
        out_shape=[pltpu.HBM(a.shape, a.dtype) for a in out_far] + list(outs),
        scratch_shapes=list(scratch) + [pltpu.SemaphoreType.DMA((copies,))] * (copies > 0),
        cost_estimate=pl.CostEstimate(flops=cost[0], bytes_accessed=cost[1], transcendentals=0),
        compiler_params=pltpu.CompilerParams(vmem_limit_bytes=32 * 1024 * 1024),
    )(*far, *near)


def like(array):
    return jax.ShapeDtypeStruct(array.shape, array.dtype)


def exchanged(value, step):
    places = lax.axis_size("head")
    return lax.ppermute(value, "head", [(i, i ^ step) for i in range(places)])


def on_device(
    hidden,
    w_qkv,
    w_out,
    s_qk,
    alpha_attn,
    w_gate_up,
    w_down,
    s_up,
    s_gate,
    alpha_mlp,
    short_keys,
    short_values,
    cache_lengths,
    long_keys,
    long_values,
    long_rows,
):
    rows, model = hidden.shape
    width = w_qkv.shape[2]
    longs = long_keys.shape[0]
    parties = lax.axis_size("req")
    shape = jax.ShapeDtypeStruct
    state = shape((rows, width), F32)
    wide = shape((rows, model), BF16)
    w_qkv, short_keys, short_values, long_keys, long_values = (
        jnp.swapaxes(a, 1, 2) for a in (w_qkv, short_keys, short_values, long_keys, long_values)
    )
    with jax.named_scope("long_hidden"):
        sent, hidden_near, match, query, gains, w_query, w_key, keys = call(
            select_kernel,
            (
                wide,
                shape((rows, 128), F32),
                state,
                like(s_qk),
                shape(w_qkv.shape[1:], BF16),
                shape(w_qkv.shape[1:], BF16),
                like(long_keys),
            ),
            (10**6, 3 * 10**6),
            far=(long_rows, hidden, s_qk, w_qkv, long_keys),
            out_far=(shape((parties, longs, model), BF16),),
            scratch=(pltpu.SMEM((longs,), jnp.int32), pltpu.VMEM((parties, longs, model), BF16)),
            copies=7,
        )
        received = lax.all_to_all(sent, "req", 0, 0)
    with jax.named_scope("short_attention"):
        short_out, short_lse, value, own, values = call(
            short_kernel,
            (state, state, state, state, like(long_values)),
            (10**9, 6 * 10**6),
            far=(cache_lengths, w_qkv, short_keys, short_values, long_values),
            near=(hidden_near, query, gains, w_key),
            scratch=(
                pltpu.SMEM((rows,), jnp.int32),
                pltpu.VMEM(w_qkv.shape[1:], BF16),
                pltpu.VMEM(short_keys.shape, BF16),
                pltpu.VMEM(short_values.shape, BF16),
            ),
            copies=5,
        )
    with jax.named_scope("long_attention"):
        partial, w_out = call(
            long_kernel,
            (shape((parties, 2 * longs, width), F32), like(w_out)),
            (10**8, 4 * 10**6),
            far=(w_out,),
            near=(received, gains, w_query, keys, values),
            copies=1,
        )
    with jax.named_scope("long_parts"):
        parts = lax.all_to_all(partial, "req", 0, 0)
    with jax.named_scope("project"):
        (projected,) = call(
            project_kernel,
            (wide,),
            (2 * rows * width * model, 10**6),
            near=(parts, short_out, short_lse, value, own, match, w_out),
        )
    with jax.named_scope("load"):
        loads = (hidden, alpha_attn, w_gate_up, w_down, s_gate, s_up, alpha_mlp)
        hidden, alpha_attn, w_gate_up, w_down, s_gate, s_up, alpha_mlp = call(
            load_kernel,
            [like(a) for a in loads],
            (10**6, 6 * 10**6),
            far=loads,
            near=(projected,),
            copies=len(loads),
        )
    with jax.named_scope("sum_heads"):
        other = exchanged(projected, 3)
        (projected,) = call(add_kernel, (wide,), (10**5, 10**5), near=(projected, other, s_up))
        other = exchanged(projected, 1)
    with jax.named_scope("mlp"):
        middle, downward = call(
            mlp_kernel,
            (wide, wide),
            (10**8, 5 * 10**6),
            near=(projected, other, hidden, alpha_attn, w_gate_up, w_down, s_gate, s_up),
        )
    with jax.named_scope("sum_units"):
        other = exchanged(downward, 3)
        (downward,) = call(add_kernel, (wide,), (10**5, 10**5), near=(downward, other))
        other = exchanged(downward, 1)
    with jax.named_scope("final"):
        (updated,) = call(
            final_kernel, (wide,), (10**6, 10**5), near=(downward, other, middle, alpha_mlp)
        )
        return updated


def solution(mesh):
    return jax.shard_map(
        on_device,
        mesh=mesh,
        in_specs=(
            P("req", None),
            P(None, None, "head"),
            P("head", None),
            P("head"),
            P(),
            P(None, None, "head"),
            P("head", None),
            P("head"),
            P("head"),
            P(),
            P("req", None, "head"),
            P("req", None, "head"),
            P("req"),
            P(None, "req", "head"),
            P(None, "req", "head"),
            P(),
        ),
        out_specs=P("req", None),
        check_vma=False,
    )
```

```python
import math

import jax
import jax.numpy as jnp
from jax import lax
from jax.experimental import pallas as pl
from jax.experimental.pallas import tpu as pltpu
from jax.sharding import PartitionSpec as P

HEAD_DIM = 64
EPS = 1e-06
LOW = -1e30
F32 = jnp.float32
BF16 = jnp.bfloat16
LANES = 8

VMEM = pl.BlockSpec(memory_space=pltpu.VMEM)
HBM = pl.BlockSpec(memory_space=pltpu.HBM)


def dot(left, right):
    return jnp.dot(left, right, preferred_element_type=F32)


def dot_t(left, right):
    return lax.dot_general(left, right, (((1,), (1,)), ((), ())), preferred_element_type=F32)


def head_masks(width):
    lane = lax.broadcasted_iota(jnp.int32, (1, width), 1)
    return [
        (lane >= h * HEAD_DIM) & (lane < (h + 1) * HEAD_DIM) for h in range(width // HEAD_DIM)
    ]


def head_rows(width):
    sub = lax.broadcasted_iota(jnp.int32, (LANES, width), 0)
    lane = lax.broadcasted_iota(jnp.int32, (LANES, width), 1)
    return (lane >= sub * HEAD_DIM) & (lane < (sub + 1) * HEAD_DIM)


def spread_sums(values, masks, function):
    result = jnp.zeros_like(values)
    for mask in masks:
        total = jnp.sum(jnp.where(mask, values, 0.0), axis=-1, keepdims=True)
        result = jnp.where(mask, function(total), result)
    return result


def head_unit(values, gains, masks):
    scale = spread_sums(values * values, masks, lambda total: lax.rsqrt(total + EPS))
    return (values * scale * gains).astype(BF16).astype(F32)


def row_norm(values):
    return values * lax.rsqrt(jnp.mean(values * values, axis=-1, keepdims=True) + EPS)


def gathered(values, diagonal):
    return jnp.sum(jnp.where(diagonal, values, 0.0), axis=0, keepdims=True)


def start_all(pairs, sems):
    copies = [pltpu.make_async_copy(s, d, sems.at[i]) for i, (s, d) in enumerate(pairs)]
    for copy in copies:
        copy.start()
    return copies


def select_kernel(
    longs_hbm,
    hidden_hbm,
    gains_hbm,
    w_hbm,
    keys_hbm,
    sent_hbm,
    hidden_ref,
    match_ref,
    query_ref,
    gains_ref,
    w_query_ref,
    w_key_ref,
    keys_ref,
    longs_ref,
    sent_ref,
    sems,
):
    copies = start_all(
        [
            (longs_hbm, longs_ref),
            (hidden_hbm, hidden_ref),
            (gains_hbm, gains_ref),
            (w_hbm.at[0], w_query_ref),
            (w_hbm.at[1], w_key_ref),
            (keys_hbm, keys_ref),
        ],
        sems,
    )
    parties, longs, _ = sent_ref.shape
    rows = hidden_ref.shape[0]
    offset = lax.axis_index("req") * rows
    sub = lax.broadcasted_iota(jnp.int32, (8, rows), 0)
    lane = lax.broadcasted_iota(jnp.int32, (8, rows), 1) + offset
    here = jnp.zeros((8, rows), jnp.bool_)
    copies[0].wait()
    for index in range(longs):
        here = here | ((sub == index) & (lane == longs_ref[index]))
    copies[1].wait()
    picked = dot(here.astype(F32).astype(BF16), hidden_ref[...])[:longs].astype(BF16)
    for party in range(parties):
        sent_ref[party] = picked
    out = pltpu.make_async_copy(sent_ref, sent_hbm, sems.at[6])
    out.start()
    row = lax.broadcasted_iota(jnp.int32, match_ref.shape, 0) + offset
    column = lax.broadcasted_iota(jnp.int32, match_ref.shape, 1)
    match = jnp.zeros(match_ref.shape, F32)
    for index in range(longs):
        match = jnp.where((row == longs_ref[index]) & (column == index), 1.0, match)
    match_ref[...] = match
    copies[2].wait()
    copies[3].wait()
    query = dot_t(hidden_ref[...], w_query_ref[...])
    query = head_unit(query, gains_ref[...][None, :], head_masks(query.shape[1]))
    query_ref[...] = query * math.sqrt(HEAD_DIM)
    copies[4].wait()
    copies[5].wait()
    out.wait()


def short_kernel(
    lengths_hbm,
    w_hbm,
    keys_hbm,
    values_hbm,
    long_values_hbm,
    hidden_ref,
    query_ref,
    gains_ref,
    w_key_ref,
    out_ref,
    lse_ref,
    value_ref,
    own_ref,
    long_values_ref,
    lengths_ref,
    w_value_ref,
    keys_ref,
    values_ref,
    sems,
):
    rows, width = out_ref.shape
    halves = [pl.ds(0, rows // 2), pl.ds(rows // 2, rows - rows // 2)]
    copies = start_all(
        [
            (lengths_hbm, lengths_ref),
            (keys_hbm.at[halves[0]], keys_ref.at[halves[0]]),
            (keys_hbm.at[halves[1]], keys_ref.at[halves[1]]),
            (w_hbm.at[2], w_value_ref),
            (values_hbm, values_ref),
            (long_values_hbm, long_values_ref),
        ],
        sems,
    )
    slots = keys_ref.shape[2]
    masks = head_masks(width)
    diagonal = head_rows(width)
    sub = lax.broadcasted_iota(jnp.int32, (2 * LANES, 2 * slots), 0)
    lane = lax.broadcasted_iota(jnp.int32, (2 * LANES, 2 * slots), 1)
    second = sub >= LANES
    first = jnp.where(second, slots, 0)
    hidden = hidden_ref[...]
    query = query_ref[...]
    pairs = [
        jnp.concatenate(
            [jnp.where(diagonal, query[r + i : r + i + 1], 0.0) for i in range(2)], axis=0
        ).astype(BF16)
        for r in range(0, rows, 2)
    ]
    key = head_unit(dot_t(hidden, w_key_ref[...]), gains_ref[...][None, :], masks)
    own_ref[...] = spread_sums(query * key, masks, lambda total: total)
    copies[0].wait()
    weights, scales = [], []
    for p, r in enumerate(range(0, rows, 2)):
        if r in (0, rows // 2):
            copies[1 + (r > 0)].wait()
        scores = dot(pairs[p], jnp.concatenate([keys_ref[r], keys_ref[r + 1]], axis=1))
        last = jnp.where(second, slots + lengths_ref[r + 1], lengths_ref[r])
        valid = (lane >= first) & (lane < last)
        scores = jnp.where(valid, scores, LOW)
        top = jnp.max(scores, axis=-1, keepdims=True)
        weight = jnp.where(valid, jnp.exp(scores - top), 0.0)
        total = jnp.sum(weight, axis=-1, keepdims=True)
        weights.append(weight.astype(BF16))
        scales.append(1.0 / total)
        lse = top + jnp.log(total)
        for i in range(2):
            part = slice(i * LANES, (i + 1) * LANES)
            lse_ref[r + i : r + i + 1, :] = gathered(lse[part], diagonal)
    copies[3].wait()
    value_ref[...] = dot_t(hidden, w_value_ref[...]).astype(BF16).astype(F32)
    copies[4].wait()
    for p, r in enumerate(range(0, rows, 2)):
        summed = dot_t(weights[p], jnp.concatenate([values_ref[r], values_ref[r + 1]], axis=1))
        summed = summed * scales[p]
        for i in range(2):
            part = slice(i * LANES, (i + 1) * LANES)
            out_ref[r + i : r + i + 1, :] = gathered(summed[part], diagonal)
    copies[5].wait()


def long_kernel(
    w_out_hbm,
    received_ref,
    gains_ref,
    w_ref,
    keys_ref,
    values_ref,
    sent_ref,
    w_out_ref,
    sems,
):
    copy = pltpu.make_async_copy(w_out_hbm, w_out_ref, sems.at[0])
    copy.start()
    parties, longs, _ = received_ref.shape
    width = w_ref.shape[0]
    hidden = received_ref[0].astype(F32)
    for party in range(1, parties):
        hidden = hidden + received_ref[party].astype(F32)
    query = dot_t(hidden.astype(BF16), w_ref[...])
    query = head_unit(query, gains_ref[...][None, :], head_masks(width)) * math.sqrt(HEAD_DIM)
    diagonal = head_rows(width)
    scores = [
        dot(jnp.where(diagonal, query[i : i + 1], 0.0).astype(BF16), keys_ref[i])
        for i in range(longs)
    ]
    outs, lses = [], []
    for i in range(longs):
        top = jnp.max(scores[i], axis=-1, keepdims=True)
        weights = jnp.exp(scores[i] - top)
        total = jnp.sum(weights, axis=-1, keepdims=True)
        summed = dot_t(weights.astype(BF16), values_ref[i])
        outs.append(gathered(summed / total, diagonal))
        lses.append(gathered(top + jnp.log(total), diagonal))
    packed = jnp.concatenate(outs + lses, axis=0)
    for party in range(parties):
        sent_ref[party] = packed
    copy.wait()


def project_kernel(
    parts_ref, short_ref, short_lse_ref, value_ref, own_ref, match_ref, w_ref, out_ref
):
    parties, doubled, width = parts_ref.shape
    longs = doubled // 2
    top = parts_ref[0]
    for party in range(1, parties):
        top = jnp.maximum(top, parts_ref[party])
    top = top[longs:]
    total = jnp.zeros((longs, width), F32)
    acc = jnp.zeros((longs, width), F32)
    for party in range(parties):
        part = parts_ref[party]
        weight = jnp.exp(part[longs:] - top)
        total = total + weight
        acc = acc + weight * part[:longs]
    long_out = acc / total
    long_lse = top + jnp.log(total)
    cached = short_ref[...]
    lse = short_lse_ref[...]
    for index in range(longs):
        here = match_ref[:, index : index + 1] > 0.5
        cached = jnp.where(here, long_out[index : index + 1], cached)
        lse = jnp.where(here, long_lse[index : index + 1], lse)
    own = own_ref[...]
    top = jnp.maximum(lse, own)
    old = jnp.exp(lse - top)
    new = jnp.exp(own - top)
    attended = (old * cached + new * value_ref[...]) / (old + new)
    out_ref[...] = dot(attended.astype(BF16), w_ref[...]).astype(BF16)


def load_kernel(*refs):
    count = (len(refs) - 2) // 2
    copies = start_all(list(zip(refs[:count], refs[count + 1 : -1])), refs[-1])
    for copy in copies:
        copy.wait()


def add_kernel(left_ref, right_ref, *refs):
    out_ref = refs[-1]
    out_ref[...] = (left_ref[...].astype(F32) + right_ref[...].astype(F32)).astype(BF16)


def renormed(left_ref, right_ref, base, alpha_ref):
    total = left_ref[...].astype(F32) + right_ref[...].astype(F32)
    alpha = alpha_ref[...][None, :]
    return row_norm(base + alpha * (row_norm(total) - base)).astype(BF16)


def mlp_kernel(
    left_ref,
    right_ref,
    hidden_ref,
    alpha_ref,
    w_gate_up_ref,
    w_down_ref,
    s_gate_ref,
    s_up_ref,
    mid_ref,
    out_ref,
):
    middle = renormed(left_ref, right_ref, hidden_ref[...].astype(F32), alpha_ref)
    mid_ref[...] = middle
    gate = dot(middle, w_gate_up_ref[0]) * s_gate_ref[...][None, :]
    upward = dot(middle, w_gate_up_ref[1]) * s_up_ref[...][None, :]
    gated = (gate / (1.0 + jnp.exp(-gate)) * upward).astype(BF16)
    out_ref[...] = dot(gated, w_down_ref[...]).astype(BF16)


def final_kernel(left_ref, right_ref, mid_ref, alpha_ref, out_ref):
    out_ref[...] = renormed(left_ref, right_ref, mid_ref[...].astype(F32), alpha_ref)


def call(kernel, outs, cost, far=(), near=(), out_far=(), scratch=(), copies=0):
    far = [pltpu.with_memory_space_constraint(a, pltpu.HBM) for a in far]
    return pl.pallas_call(
        kernel,
        in_specs=[HBM] * len(far) + [VMEM] * len(near),
        out_specs=[HBM] * len(out_far) + [VMEM] * len(outs),
        out_shape=[pltpu.HBM(a.shape, a.dtype) for a in out_far] + list(outs),
        scratch_shapes=list(scratch) + [pltpu.SemaphoreType.DMA((copies,))] * (copies > 0),
        cost_estimate=pl.CostEstimate(flops=cost[0], bytes_accessed=cost[1], transcendentals=0),
        compiler_params=pltpu.CompilerParams(vmem_limit_bytes=32 * 1024 * 1024),
    )(*far, *near)


def like(array):
    return jax.ShapeDtypeStruct(array.shape, array.dtype)


def mixed_groups(parties):
    places = lax.axis_size("head")
    return [
        [r * places + (h ^ ((r // 2) % 2)) for r in range(parties)] for h in range(places)
    ]


def exchanged(value, step):
    places = lax.axis_size("head")
    return lax.ppermute(value, "head", [(i, i ^ step) for i in range(places)])


def on_device(
    hidden,
    w_qkv,
    w_out,
    s_qk,
    alpha_attn,
    w_gate_up,
    w_down,
    s_up,
    s_gate,
    alpha_mlp,
    short_keys,
    short_values,
    cache_lengths,
    long_keys,
    long_values,
    long_rows,
):
    rows, model = hidden.shape
    width = w_qkv.shape[2]
    longs = long_keys.shape[0]
    parties = lax.axis_size("req")
    shape = jax.ShapeDtypeStruct
    state = shape((rows, width), F32)
    wide = shape((rows, model), BF16)
    w_qkv, short_keys, short_values, long_keys, long_values = (
        jnp.swapaxes(a, 1, 2) for a in (w_qkv, short_keys, short_values, long_keys, long_values)
    )
    with jax.named_scope("long_hidden"):
        sent, hidden_near, match, query, gains, w_query, w_key, keys = call(
            select_kernel,
            (
                wide,
                shape((rows, 128), F32),
                state,
                like(s_qk),
                shape(w_qkv.shape[1:], BF16),
                shape(w_qkv.shape[1:], BF16),
                like(long_keys),
            ),
            (10**6, 3 * 10**6),
            far=(long_rows, hidden, s_qk, w_qkv, long_keys),
            out_far=(shape((parties, longs, model), BF16),),
            scratch=(pltpu.SMEM((longs,), jnp.int32), pltpu.VMEM((parties, longs, model), BF16)),
            copies=7,
        )
        received = lax.all_to_all(
            sent, ("req", "head"), 0, 0, axis_index_groups=mixed_groups(parties)
        )
    with jax.named_scope("short_attention"):
        short_out, short_lse, value, own, values = call(
            short_kernel,
            (state, state, state, state, like(long_values)),
            (10**9, 6 * 10**6),
            far=(cache_lengths, w_qkv, short_keys, short_values, long_values),
            near=(hidden_near, query, gains, w_key),
            scratch=(
                pltpu.SMEM((rows,), jnp.int32),
                pltpu.VMEM(w_qkv.shape[1:], BF16),
                pltpu.VMEM(short_keys.shape, BF16),
                pltpu.VMEM(short_values.shape, BF16),
            ),
            copies=6,
        )
    with jax.named_scope("long_attention"):
        partial, w_out = call(
            long_kernel,
            (shape((parties, 2 * longs, width), F32), like(w_out)),
            (10**8, 4 * 10**6),
            far=(w_out,),
            near=(received, gains, w_query, keys, values),
            copies=1,
        )
    with jax.named_scope("long_parts"):
        parts = lax.all_to_all(partial, "req", 0, 0)
    with jax.named_scope("project"):
        (projected,) = call(
            project_kernel,
            (wide,),
            (2 * rows * width * model, 10**6),
            near=(parts, short_out, short_lse, value, own, match, w_out),
        )
    with jax.named_scope("load"):
        loads = (hidden, alpha_attn, w_gate_up, w_down, s_gate, s_up, alpha_mlp)
        hidden, alpha_attn, w_gate_up, w_down, s_gate, s_up, alpha_mlp = call(
            load_kernel,
            [like(a) for a in loads],
            (10**6, 6 * 10**6),
            far=loads,
            near=(projected,),
            copies=len(loads),
        )
    with jax.named_scope("sum_heads"):
        other = exchanged(projected, 3)
        (projected,) = call(add_kernel, (wide,), (10**5, 10**5), near=(projected, other, s_up))
        other = exchanged(projected, 1)
    with jax.named_scope("mlp"):
        middle, downward = call(
            mlp_kernel,
            (wide, wide),
            (10**8, 5 * 10**6),
            near=(projected, other, hidden, alpha_attn, w_gate_up, w_down, s_gate, s_up),
        )
    with jax.named_scope("sum_units"):
        other = exchanged(downward, 3)
        (downward,) = call(add_kernel, (wide,), (10**5, 10**5), near=(downward, other))
        other = exchanged(downward, 1)
    with jax.named_scope("final"):
        (updated,) = call(
            final_kernel, (wide,), (10**6, 10**5), near=(downward, other, middle, alpha_mlp)
        )
        return updated


def solution(mesh):
    return jax.shard_map(
        on_device,
        mesh=mesh,
        in_specs=(
            P("req", None),
            P(None, None, "head"),
            P("head", None),
            P("head"),
            P(),
            P(None, None, "head"),
            P("head", None),
            P("head"),
            P("head"),
            P(),
            P("req", None, "head"),
            P("req", None, "head"),
            P("req"),
            P(None, "req", "head"),
            P(None, "req", "head"),
            P(),
        ),
        out_specs=P("req", None),
        check_vma=False,
    )
```

```python
import math

import jax
import jax.numpy as jnp
from jax import lax
from jax.experimental import pallas as pl
from jax.experimental.pallas import tpu as pltpu
from jax.sharding import PartitionSpec as P

HEAD_DIM = 64
EPS = 1e-06
LOW = -3e38
F32 = jnp.float32
BF16 = jnp.bfloat16
LANES = 8

VMEM = pl.BlockSpec(memory_space=pltpu.VMEM)
HBM = pl.BlockSpec(memory_space=pltpu.HBM)


def dot(left, right):
    return jnp.dot(left, right, preferred_element_type=F32)


def dot_t(left, right):
    return lax.dot_general(left, right, (((1,), (1,)), ((), ())), preferred_element_type=F32)


def head_masks(width):
    lane = lax.broadcasted_iota(jnp.int32, (1, width), 1)
    return [
        (lane >= h * HEAD_DIM) & (lane < (h + 1) * HEAD_DIM) for h in range(width // HEAD_DIM)
    ]


def head_rows(width):
    sub = lax.broadcasted_iota(jnp.int32, (LANES, width), 0)
    lane = lax.broadcasted_iota(jnp.int32, (LANES, width), 1)
    return (lane >= sub * HEAD_DIM) & (lane < (sub + 1) * HEAD_DIM)


def spread_sums(values, masks, function):
    result = jnp.zeros_like(values)
    for mask in masks:
        total = jnp.sum(jnp.where(mask, values, 0.0), axis=-1, keepdims=True)
        result = jnp.where(mask, function(total), result)
    return result


def head_unit(values, gains, masks):
    scale = spread_sums(values * values, masks, lambda total: lax.rsqrt(total + EPS))
    return (values * scale * gains).astype(BF16).astype(F32)


def row_norm(values):
    return values * lax.rsqrt(jnp.mean(values * values, axis=-1, keepdims=True) + EPS)


def gathered(values, diagonal):
    return jnp.sum(jnp.where(diagonal, values, 0.0), axis=0, keepdims=True)


def start_all(pairs, sems):
    copies = [pltpu.make_async_copy(s, d, sems.at[i]) for i, (s, d) in enumerate(pairs)]
    for copy in copies:
        copy.start()
    return copies


def select_kernel(
    longs_hbm,
    hidden_hbm,
    gains_hbm,
    w_hbm,
    keys_hbm,
    sent_hbm,
    hidden_ref,
    match_ref,
    query_ref,
    gains_ref,
    w_query_ref,
    w_key_ref,
    keys_ref,
    longs_ref,
    sent_ref,
    sems,
):
    copies = start_all(
        [
            (longs_hbm, longs_ref),
            (hidden_hbm, hidden_ref),
            (gains_hbm, gains_ref),
            (w_hbm.at[0], w_query_ref),
            (w_hbm.at[1], w_key_ref),
            (keys_hbm, keys_ref),
        ],
        sems,
    )
    parties, longs, _ = sent_ref.shape
    rows = hidden_ref.shape[0]
    offset = lax.axis_index("req") * rows
    sub = lax.broadcasted_iota(jnp.int32, (8, rows), 0)
    lane = lax.broadcasted_iota(jnp.int32, (8, rows), 1) + offset
    here = jnp.zeros((8, rows), jnp.bool_)
    copies[0].wait()
    for index in range(longs):
        here = here | ((sub == index) & (lane == longs_ref[index]))
    copies[1].wait()
    picked = dot(here.astype(F32).astype(BF16), hidden_ref[...])[:longs].astype(BF16)
    for party in range(parties):
        sent_ref[party] = picked
    out = pltpu.make_async_copy(sent_ref, sent_hbm, sems.at[6])
    out.start()
    row = lax.broadcasted_iota(jnp.int32, match_ref.shape, 0) + offset
    column = lax.broadcasted_iota(jnp.int32, match_ref.shape, 1)
    match = jnp.zeros(match_ref.shape, F32)
    for index in range(longs):
        match = jnp.where((row == longs_ref[index]) & (column == index), 1.0, match)
    match_ref[...] = match
    copies[2].wait()
    copies[3].wait()
    query = dot_t(hidden_ref[...], w_query_ref[...])
    query = head_unit(query, gains_ref[...][None, :], head_masks(query.shape[1]))
    query_ref[...] = query * math.sqrt(HEAD_DIM)
    copies[4].wait()
    copies[5].wait()
    out.wait()


def short_kernel(
    lengths_hbm,
    w_hbm,
    keys_hbm,
    values_hbm,
    long_values_hbm,
    hidden_ref,
    query_ref,
    gains_ref,
    w_key_ref,
    out_ref,
    lse_ref,
    value_ref,
    own_ref,
    long_values_ref,
    lengths_ref,
    w_value_ref,
    keys_ref,
    values_ref,
    sems,
):
    rows, width = out_ref.shape
    halves = [pl.ds(0, rows // 2), pl.ds(rows // 2, rows - rows // 2)]
    copies = start_all(
        [
            (lengths_hbm, lengths_ref),
            (keys_hbm.at[halves[0]], keys_ref.at[halves[0]]),
            (keys_hbm.at[halves[1]], keys_ref.at[halves[1]]),
            (w_hbm.at[2], w_value_ref),
            (values_hbm, values_ref),
            (long_values_hbm, long_values_ref),
        ],
        sems,
    )
    @pl.when(lax.axis_index("req") >= 0)
    def _():
        slots = keys_ref.shape[2]
        masks = head_masks(width)
        diagonal = head_rows(width)
        sub = lax.broadcasted_iota(jnp.int32, (2 * LANES, 2 * slots), 0)
        lane = lax.broadcasted_iota(jnp.int32, (2 * LANES, 2 * slots), 1)
        second = sub >= LANES
        first = jnp.where(second, slots, 0)
        hidden = hidden_ref[...]
        query = query_ref[...]
        pairs = [
            jnp.concatenate(
                [jnp.where(diagonal, query[r + i : r + i + 1], 0.0) for i in range(2)], axis=0
            ).astype(BF16)
            for r in range(0, rows, 2)
        ]
        key = head_unit(dot_t(hidden, w_key_ref[...]), gains_ref[...][None, :], masks)
        own_ref[...] = spread_sums(query * key, masks, lambda total: total)
        copies[0].wait()
        weights, scales = [], []
        for p, r in enumerate(range(0, rows, 2)):
            if r in (0, rows // 2):
                copies[1 + (r > 0)].wait()
            scores = dot(pairs[p], jnp.concatenate([keys_ref[r], keys_ref[r + 1]], axis=1))
            last = jnp.where(second, slots + lengths_ref[r + 1], lengths_ref[r])
            valid = (lane >= first) & (lane < last)
            scores = jnp.where(valid, scores, LOW)
            top = jnp.max(scores, axis=-1, keepdims=True)
            weight = jnp.where(valid, jnp.exp(scores - top), 0.0)
            total = jnp.sum(weight, axis=-1, keepdims=True)
            weights.append(weight.astype(BF16))
            scales.append(1.0 / total)
            lse = top + jnp.log(total)
            for i in range(2):
                part = slice(i * LANES, (i + 1) * LANES)
                lse_ref[r + i : r + i + 1, :] = gathered(lse[part], diagonal)
        copies[3].wait()
        value_ref[...] = dot_t(hidden, w_value_ref[...]).astype(BF16).astype(F32)
        copies[4].wait()
        for p, r in enumerate(range(0, rows, 2)):
            summed = dot_t(weights[p], jnp.concatenate([values_ref[r], values_ref[r + 1]], axis=1))
            summed = summed * scales[p]
            for i in range(2):
                part = slice(i * LANES, (i + 1) * LANES)
                out_ref[r + i : r + i + 1, :] = gathered(summed[part], diagonal)
        copies[5].wait()


def long_kernel(
    received_ref,
    gains_ref,
    w_ref,
    keys_ref,
    values_ref,
    sent_ref,
):
    parties, longs, _ = received_ref.shape
    width = w_ref.shape[0]
    hidden = received_ref[0].astype(F32)
    for party in range(1, parties):
        hidden = hidden + received_ref[party].astype(F32)
    query = dot_t(hidden.astype(BF16), w_ref[...])
    query = head_unit(query, gains_ref[...][None, :], head_masks(width)) * math.sqrt(HEAD_DIM)
    diagonal = head_rows(width)
    scores = [
        dot(jnp.where(diagonal, query[i : i + 1], 0.0).astype(BF16), keys_ref[i])
        for i in range(longs)
    ]
    padded = sent_ref.shape[2]
    sub = lax.broadcasted_iota(jnp.int32, (LANES, padded), 0)
    lane = lax.broadcasted_iota(jnp.int32, (LANES, padded), 1)
    kept = ((lane >= sub * HEAD_DIM) & (lane < (sub + 1) * HEAD_DIM) & (lane < width)) | (
        lane == width + sub
    )
    outs = []
    for i in range(longs):
        top = jnp.max(scores[i], axis=-1, keepdims=True)
        weights = jnp.exp(scores[i] - top)
        total = jnp.sum(weights, axis=-1, keepdims=True)
        summed = dot_t(weights.astype(BF16), values_ref[i]) / total
        summed = jnp.concatenate([summed, jnp.zeros((LANES, padded - width), F32)], axis=1)
        row = jnp.where(lane < width, summed, top + jnp.log(total))
        outs.append(jnp.sum(jnp.where(kept, row, 0.0), axis=0, keepdims=True))
    packed = jnp.concatenate(outs, axis=0)
    for party in range(parties):
        sent_ref[party] = packed


def project_kernel(
    parts_ref, short_ref, short_lse_ref, value_ref, own_ref, match_ref, w_ref, out_ref
):
    parties, longs, padded = parts_ref.shape
    width = short_ref.shape[1]
    masks = head_masks(width)
    last = padded - 128
    first = width - last

    def on_heads(compact):
        result = jnp.zeros((longs, width), F32)
        for h, mask in enumerate(masks):
            result = jnp.where(mask, compact[:, first + h : first + h + 1], result)
        return result

    lses = [parts_ref[party][:, last:] for party in range(parties)]
    top = lses[0]
    for lse in lses[1:]:
        top = jnp.maximum(top, lse)
    weights = [jnp.exp(lse - top) for lse in lses]
    total = weights[0]
    for weight in weights[1:]:
        total = total + weight
    long_out = jnp.zeros((longs, width), F32)
    for party in range(parties):
        long_out = long_out + on_heads(weights[party] / total) * parts_ref[party][:, :width]
    long_lse = on_heads(top + jnp.log(total))
    cached = short_ref[...]
    lse = short_lse_ref[...]
    for index in range(longs):
        here = match_ref[:, index : index + 1] > 0.5
        cached = jnp.where(here, long_out[index : index + 1], cached)
        lse = jnp.where(here, long_lse[index : index + 1], lse)
    own = own_ref[...]
    top = jnp.maximum(lse, own)
    old = jnp.exp(lse - top)
    new = jnp.exp(own - top)
    attended = (old * cached + new * value_ref[...]) / (old + new)
    out_ref[...] = dot(attended.astype(BF16), w_ref[...]).astype(BF16)


def add_kernel(left_ref, right_ref, out_ref):
    out_ref[...] = (left_ref[...].astype(F32) + right_ref[...].astype(F32)).astype(BF16)


def renormed(left_ref, right_ref, base, alpha_ref):
    total = left_ref[...].astype(F32) + right_ref[...].astype(F32)
    alpha = alpha_ref[...][None, :]
    return row_norm(base + alpha * (row_norm(total) - base)).astype(BF16)


def mlp_kernel(
    left_ref,
    right_ref,
    hidden_ref,
    alpha_ref,
    w_gate_up_ref,
    w_down_ref,
    s_gate_ref,
    s_up_ref,
    mid_ref,
    out_ref,
):
    middle = renormed(left_ref, right_ref, hidden_ref[...].astype(F32), alpha_ref)
    mid_ref[...] = middle
    gate = dot(middle, w_gate_up_ref[0]) * s_gate_ref[...][None, :]
    upward = dot(middle, w_gate_up_ref[1]) * s_up_ref[...][None, :]
    gated = (gate / (1.0 + jnp.exp(-gate)) * upward).astype(BF16)
    out_ref[...] = dot(gated, w_down_ref[...]).astype(BF16)


def final_kernel(left_ref, right_ref, mid_ref, alpha_ref, out_ref):
    out_ref[...] = renormed(left_ref, right_ref, mid_ref[...].astype(F32), alpha_ref)


def call(kernel, outs, cost, far=(), near=(), out_far=(), scratch=(), copies=0):
    far = [pltpu.with_memory_space_constraint(a, pltpu.HBM) for a in far]
    return pl.pallas_call(
        kernel,
        in_specs=[HBM] * len(far) + [VMEM] * len(near),
        out_specs=[HBM] * len(out_far) + [VMEM] * len(outs),
        out_shape=[pltpu.HBM(a.shape, a.dtype) for a in out_far] + list(outs),
        scratch_shapes=list(scratch) + [pltpu.SemaphoreType.DMA((copies,))] * (copies > 0),
        cost_estimate=pl.CostEstimate(flops=cost[0], bytes_accessed=cost[1], transcendentals=0),
        compiler_params=pltpu.CompilerParams(vmem_limit_bytes=32 * 1024 * 1024),
    )(*far, *near)


def like(array):
    return jax.ShapeDtypeStruct(array.shape, array.dtype)


def mixed_groups(parties):
    places = lax.axis_size("head")
    return [
        [r * places + (h ^ ((r // 2) % 2)) for r in range(parties)] for h in range(places)
    ]


def exchanged(value, step):
    places = lax.axis_size("head")
    return lax.ppermute(value, "head", [(i, i ^ step) for i in range(places)])


def on_device(
    hidden,
    w_qkv,
    w_out,
    s_qk,
    alpha_attn,
    w_gate_up,
    w_down,
    s_up,
    s_gate,
    alpha_mlp,
    short_keys,
    short_values,
    cache_lengths,
    long_keys,
    long_values,
    long_rows,
):
    rows, model = hidden.shape
    width = w_qkv.shape[2]
    longs = long_keys.shape[0]
    parties = lax.axis_size("req")
    shape = jax.ShapeDtypeStruct
    state = shape((rows, width), F32)
    wide = shape((rows, model), BF16)
    w_qkv, short_keys, short_values, long_keys, long_values = (
        jnp.swapaxes(a, 1, 2) for a in (w_qkv, short_keys, short_values, long_keys, long_values)
    )
    with jax.named_scope("long_hidden"):
        sent, hidden_near, match, query, gains, w_query, w_key, keys = call(
            select_kernel,
            (
                wide,
                shape((rows, 128), F32),
                state,
                like(s_qk),
                shape(w_qkv.shape[1:], BF16),
                shape(w_qkv.shape[1:], BF16),
                like(long_keys),
            ),
            (10**6, 3 * 10**6),
            far=(long_rows, hidden, s_qk, w_qkv, long_keys),
            out_far=(shape((parties, longs, model), BF16),),
            scratch=(pltpu.SMEM((longs,), jnp.int32), pltpu.VMEM((parties, longs, model), BF16)),
            copies=7,
        )
        received = lax.all_to_all(
            sent, ("req", "head"), 0, 0, axis_index_groups=mixed_groups(parties)
        )
    with jax.named_scope("short_attention"):
        short_out, short_lse, value, own, values = call(
            short_kernel,
            (state, state, state, state, like(long_values)),
            (10**9, 6 * 10**6),
            far=(cache_lengths, w_qkv, short_keys, short_values, long_values),
            near=(hidden_near, query, gains, w_key),
            scratch=(
                pltpu.SMEM((rows,), jnp.int32),
                pltpu.VMEM(w_qkv.shape[1:], BF16),
                pltpu.VMEM(short_keys.shape, BF16),
                pltpu.VMEM(short_values.shape, BF16),
            ),
            copies=6,
        )
    with jax.named_scope("long_attention"):
        (partial,) = call(
            long_kernel,
            (shape((parties, longs, (width // 128 + 1) * 128), F32),),
            (10**9, 4 * 10**6),
            near=(received, gains, w_query, keys, values),
        )
    with jax.named_scope("long_parts"):
        parts = lax.all_to_all(partial, "req", 0, 0)
    with jax.named_scope("project"):
        (projected,) = call(
            project_kernel,
            (wide,),
            (2 * 10**10, 10**6),
            near=(parts, short_out, short_lse, value, own, match, w_out),
        )
    with jax.named_scope("sum_heads"):
        other = exchanged(projected, 1)
        (projected,) = call(add_kernel, (wide,), (10**5, 10**5), near=(projected, other))
        other = exchanged(projected, 3)
    with jax.named_scope("mlp"):
        middle, downward = call(
            mlp_kernel,
            (wide, wide),
            (10**8, 5 * 10**6),
            near=(projected, other, hidden, alpha_attn, w_gate_up, w_down, s_gate, s_up),
        )
    with jax.named_scope("sum_units"):
        other = exchanged(downward, 3)
        (downward,) = call(add_kernel, (wide,), (10**5, 10**5), near=(downward, other))
        other = exchanged(downward, 1)
    with jax.named_scope("final"):
        (updated,) = call(
            final_kernel, (wide,), (10**6, 10**5), near=(downward, other, middle, alpha_mlp)
        )
        return updated


def solution(mesh):
    return jax.shard_map(
        on_device,
        mesh=mesh,
        in_specs=(
            P("req", None),
            P(None, None, "head"),
            P("head", None),
            P("head"),
            P(),
            P(None, None, "head"),
            P("head", None),
            P("head"),
            P("head"),
            P(),
            P("req", None, "head"),
            P("req", None, "head"),
            P("req"),
            P(None, "req", "head"),
            P(None, "req", "head"),
            P(),
        ),
        out_specs=P("req", None),
        check_vma=False,
    )
```

```python
import math

import jax
import jax.numpy as jnp
from jax import lax
from jax.experimental import pallas as pl
from jax.experimental.pallas import tpu as pltpu
from jax.sharding import PartitionSpec as P

HEAD_DIM = 64
EPS = 1e-06
LOW = -3e38
F32 = jnp.float32
BF16 = jnp.bfloat16
LANES = 8

VMEM = pl.BlockSpec(memory_space=pltpu.VMEM)
HBM = pl.BlockSpec(memory_space=pltpu.HBM)


def dot(left, right):
    return jnp.dot(left, right, preferred_element_type=F32)


def dot_t(left, right):
    return lax.dot_general(left, right, (((1,), (1,)), ((), ())), preferred_element_type=F32)


def head_masks(width):
    lane = lax.broadcasted_iota(jnp.int32, (1, width), 1)
    return [
        (lane >= h * HEAD_DIM) & (lane < (h + 1) * HEAD_DIM) for h in range(width // HEAD_DIM)
    ]


def head_rows(width):
    sub = lax.broadcasted_iota(jnp.int32, (LANES, width), 0)
    lane = lax.broadcasted_iota(jnp.int32, (LANES, width), 1)
    return (lane >= sub * HEAD_DIM) & (lane < (sub + 1) * HEAD_DIM)


def spread_sums(values, masks, function):
    result = jnp.zeros_like(values)
    for mask in masks:
        total = jnp.sum(jnp.where(mask, values, 0.0), axis=-1, keepdims=True)
        result = jnp.where(mask, function(total), result)
    return result


def head_unit(values, gains, masks):
    scale = spread_sums(values * values, masks, lambda total: lax.rsqrt(total + EPS))
    return (values * scale * gains).astype(BF16).astype(F32)


def row_norm(values):
    return values * lax.rsqrt(jnp.mean(values * values, axis=-1, keepdims=True) + EPS)


def gathered(values, diagonal):
    return jnp.sum(jnp.where(diagonal, values, 0.0), axis=0, keepdims=True)


def start_all(pairs, sems):
    copies = [pltpu.make_async_copy(s, d, sems.at[i]) for i, (s, d) in enumerate(pairs)]
    for copy in copies:
        copy.start()
    return copies


def select_kernel(
    longs_hbm,
    hidden_hbm,
    gains_hbm,
    w_hbm,
    keys_hbm,
    sent_hbm,
    hidden_ref,
    match_ref,
    query_ref,
    gains_ref,
    w_query_ref,
    w_key_ref,
    keys_ref,
    longs_ref,
    sent_ref,
    sems,
):
    copies = start_all(
        [
            (longs_hbm, longs_ref),
            (hidden_hbm, hidden_ref),
            (gains_hbm, gains_ref),
            (w_hbm.at[0], w_query_ref),
            (w_hbm.at[1], w_key_ref),
            (keys_hbm, keys_ref),
        ],
        sems,
    )
    parties, longs, _ = sent_ref.shape
    rows = hidden_ref.shape[0]
    offset = lax.axis_index("req") * rows
    sub = lax.broadcasted_iota(jnp.int32, (8, rows), 0)
    lane = lax.broadcasted_iota(jnp.int32, (8, rows), 1) + offset
    here = jnp.zeros((8, rows), jnp.bool_)
    copies[0].wait()
    for index in range(longs):
        here = here | ((sub == index) & (lane == longs_ref[index]))
    copies[1].wait()
    picked = dot(here.astype(F32).astype(BF16), hidden_ref[...])[:longs].astype(BF16)
    for party in range(parties):
        sent_ref[party] = picked
    out = pltpu.make_async_copy(sent_ref, sent_hbm, sems.at[6])
    out.start()
    row = lax.broadcasted_iota(jnp.int32, match_ref.shape, 0) + offset
    column = lax.broadcasted_iota(jnp.int32, match_ref.shape, 1)
    match = jnp.zeros(match_ref.shape, F32)
    for index in range(longs):
        match = jnp.where((row == longs_ref[index]) & (column == index), 1.0, match)
    match_ref[...] = match
    copies[2].wait()
    copies[3].wait()
    query = dot_t(hidden_ref[...], w_query_ref[...])
    query = head_unit(query, gains_ref[...][None, :], head_masks(query.shape[1]))
    query_ref[...] = query * math.sqrt(HEAD_DIM)
    copies[4].wait()
    copies[5].wait()
    out.wait()


def short_kernel(
    lengths_hbm,
    w_hbm,
    keys_hbm,
    values_hbm,
    long_values_hbm,
    hidden_ref,
    query_ref,
    gains_ref,
    w_key_ref,
    out_ref,
    lse_ref,
    value_ref,
    own_ref,
    long_values_ref,
    lengths_ref,
    w_value_ref,
    keys_ref,
    values_ref,
    sems,
):
    rows, width = out_ref.shape
    halves = [pl.ds(0, rows // 2), pl.ds(rows // 2, rows - rows // 2)]
    copies = start_all(
        [
            (lengths_hbm, lengths_ref),
            (keys_hbm.at[halves[0]], keys_ref.at[halves[0]]),
            (keys_hbm.at[halves[1]], keys_ref.at[halves[1]]),
            (w_hbm.at[2], w_value_ref),
            (values_hbm, values_ref),
            (long_values_hbm, long_values_ref),
        ],
        sems,
    )
    @pl.when(lax.axis_index("req") >= 0)
    def _():
        slots = keys_ref.shape[2]
        masks = head_masks(width)
        diagonal = head_rows(width)
        sub = lax.broadcasted_iota(jnp.int32, (2 * LANES, 2 * slots), 0)
        lane = lax.broadcasted_iota(jnp.int32, (2 * LANES, 2 * slots), 1)
        second = sub >= LANES
        first = jnp.where(second, slots, 0)
        hidden = hidden_ref[...]
        query = query_ref[...]
        pairs = [
            jnp.concatenate(
                [jnp.where(diagonal, query[r + i : r + i + 1], 0.0) for i in range(2)], axis=0
            ).astype(BF16)
            for r in range(0, rows, 2)
        ]
        key = head_unit(dot_t(hidden, w_key_ref[...]), gains_ref[...][None, :], masks)
        own_ref[...] = spread_sums(query * key, masks, lambda total: total)
        copies[0].wait()
        weights, scales = [], []
        for p, r in enumerate(range(0, rows, 2)):
            if r in (0, rows // 2):
                copies[1 + (r > 0)].wait()
            scores = dot(pairs[p], jnp.concatenate([keys_ref[r], keys_ref[r + 1]], axis=1))
            last = jnp.where(second, slots + lengths_ref[r + 1], lengths_ref[r])
            valid = (lane >= first) & (lane < last)
            scores = jnp.where(valid, scores, LOW)
            top = jnp.max(scores, axis=-1, keepdims=True)
            weight = jnp.where(valid, jnp.exp(scores - top), 0.0)
            total = jnp.sum(weight, axis=-1, keepdims=True)
            weights.append(weight.astype(BF16))
            scales.append(1.0 / total)
            lse = top + jnp.log(total)
            for i in range(2):
                part = slice(i * LANES, (i + 1) * LANES)
                lse_ref[r + i : r + i + 1, :] = gathered(lse[part], diagonal)
        copies[3].wait()
        value_ref[...] = dot_t(hidden, w_value_ref[...]).astype(BF16).astype(F32)
        copies[4].wait()
        for p, r in enumerate(range(0, rows, 2)):
            summed = dot_t(weights[p], jnp.concatenate([values_ref[r], values_ref[r + 1]], axis=1))
            summed = summed * scales[p]
            for i in range(2):
                part = slice(i * LANES, (i + 1) * LANES)
                out_ref[r + i : r + i + 1, :] = gathered(summed[part], diagonal)
        copies[5].wait()


def long_kernel(
    received_ref,
    gains_ref,
    w_ref,
    keys_ref,
    values_ref,
    sent_ref,
):
    parties, longs, _ = received_ref.shape
    width = w_ref.shape[0]
    hidden = received_ref[0].astype(F32)
    for party in range(1, parties):
        hidden = hidden + received_ref[party].astype(F32)
    query = dot_t(hidden.astype(BF16), w_ref[...])
    query = head_unit(query, gains_ref[...][None, :], head_masks(width)) * math.sqrt(HEAD_DIM)
    diagonal = head_rows(width)
    scores = [
        dot(jnp.where(diagonal, query[i : i + 1], 0.0).astype(BF16), keys_ref[i])
        for i in range(longs)
    ]
    padded = sent_ref.shape[2]
    sub = lax.broadcasted_iota(jnp.int32, (LANES, padded), 0)
    lane = lax.broadcasted_iota(jnp.int32, (LANES, padded), 1)
    kept = ((lane >= sub * HEAD_DIM) & (lane < (sub + 1) * HEAD_DIM) & (lane < width)) | (
        lane == width + sub
    )
    outs = []
    for i in range(longs):
        top = jnp.max(scores[i], axis=-1, keepdims=True)
        weights = jnp.exp(scores[i] - top)
        total = jnp.sum(weights, axis=-1, keepdims=True)
        summed = dot_t(weights.astype(BF16), values_ref[i]) / total
        summed = jnp.concatenate([summed, jnp.zeros((LANES, padded - width), F32)], axis=1)
        row = jnp.where(lane < width, summed, top + jnp.log(total))
        outs.append(jnp.sum(jnp.where(kept, row, 0.0), axis=0, keepdims=True))
    packed = jnp.concatenate(outs, axis=0)
    for party in range(parties):
        sent_ref[party] = packed


def project_kernel(
    parts_ref, short_ref, short_lse_ref, value_ref, own_ref, match_ref, w_ref, out_ref
):
    parties, longs, padded = parts_ref.shape
    width = short_ref.shape[1]
    masks = head_masks(width)
    last = padded - 128
    first = width - last

    def on_heads(compact):
        result = jnp.zeros((longs, width), F32)
        for h, mask in enumerate(masks):
            result = jnp.where(mask, compact[:, first + h : first + h + 1], result)
        return result

    lses = [parts_ref[party][:, last:] for party in range(parties)]
    top = lses[0]
    for lse in lses[1:]:
        top = jnp.maximum(top, lse)
    weights = [jnp.exp(lse - top) for lse in lses]
    total = weights[0]
    for weight in weights[1:]:
        total = total + weight
    long_out = jnp.zeros((longs, width), F32)
    for party in range(parties):
        long_out = long_out + on_heads(weights[party] / total) * parts_ref[party][:, :width]
    long_lse = on_heads(top + jnp.log(total))
    cached = short_ref[...]
    lse = short_lse_ref[...]
    for index in range(longs):
        here = match_ref[:, index : index + 1] > 0.5
        cached = jnp.where(here, long_out[index : index + 1], cached)
        lse = jnp.where(here, long_lse[index : index + 1], lse)
    own = own_ref[...]
    top = jnp.maximum(lse, own)
    old = jnp.exp(lse - top)
    new = jnp.exp(own - top)
    attended = (old * cached + new * value_ref[...]) / (old + new)
    out_ref[...] = dot(attended.astype(BF16), w_ref[...]).astype(BF16)


def add_kernel(left_ref, right_ref, out_ref):
    out_ref[...] = (left_ref[...].astype(F32) + right_ref[...].astype(F32)).astype(BF16)


def renormed(left_ref, right_ref, base, alpha_ref):
    total = left_ref[...].astype(F32) + right_ref[...].astype(F32)
    alpha = alpha_ref[...][None, :]
    return row_norm(base + alpha * (row_norm(total) - base)).astype(BF16)


def mlp_kernel(
    left_ref,
    right_ref,
    hidden_ref,
    alpha_ref,
    w_gate_up_ref,
    w_down_ref,
    s_gate_ref,
    s_up_ref,
    mid_ref,
    out_ref,
):
    middle = renormed(left_ref, right_ref, hidden_ref[...].astype(F32), alpha_ref)
    mid_ref[...] = middle
    gate = dot(middle, w_gate_up_ref[0]) * s_gate_ref[...][None, :]
    upward = dot(middle, w_gate_up_ref[1]) * s_up_ref[...][None, :]
    gated = (gate / (1.0 + jnp.exp(-gate)) * upward).astype(BF16)
    out_ref[...] = dot(gated, w_down_ref[...]).astype(BF16)


def final_kernel(left_ref, right_ref, mid_ref, alpha_ref, out_ref):
    out_ref[...] = renormed(left_ref, right_ref, mid_ref[...].astype(F32), alpha_ref)


def call(kernel, outs, cost, far=(), near=(), out_far=(), scratch=(), copies=0):
    far = [pltpu.with_memory_space_constraint(a, pltpu.HBM) for a in far]
    return pl.pallas_call(
        kernel,
        in_specs=[HBM] * len(far) + [VMEM] * len(near),
        out_specs=[HBM] * len(out_far) + [VMEM] * len(outs),
        out_shape=[pltpu.HBM(a.shape, a.dtype) for a in out_far] + list(outs),
        scratch_shapes=list(scratch) + [pltpu.SemaphoreType.DMA((copies,))] * (copies > 0),
        cost_estimate=pl.CostEstimate(flops=cost[0], bytes_accessed=cost[1], transcendentals=0),
        compiler_params=pltpu.CompilerParams(vmem_limit_bytes=32 * 1024 * 1024),
    )(*far, *near)


def like(array):
    return jax.ShapeDtypeStruct(array.shape, array.dtype)


def centre_first(parties):
    return sorted(range(parties), key=lambda r: (r != parties // 2, r))


def mixed_groups(parties):
    places = lax.axis_size("head")
    return [
        [r * places + (h ^ ((r // 2) % 2)) for r in centre_first(parties)] for h in range(places)
    ]


def exchanged(value, step):
    places = lax.axis_size("head")
    return lax.ppermute(value, "head", [(i, i ^ step) for i in range(places)])


def on_device(
    hidden,
    w_qkv,
    w_out,
    s_qk,
    alpha_attn,
    w_gate_up,
    w_down,
    s_up,
    s_gate,
    alpha_mlp,
    short_keys,
    short_values,
    cache_lengths,
    long_keys,
    long_values,
    long_rows,
):
    rows, model = hidden.shape
    width = w_qkv.shape[2]
    longs = long_keys.shape[0]
    parties = lax.axis_size("req")
    shape = jax.ShapeDtypeStruct
    state = shape((rows, width), F32)
    wide = shape((rows, model), BF16)
    w_qkv, short_keys, short_values, long_keys, long_values = (
        jnp.swapaxes(a, 1, 2) for a in (w_qkv, short_keys, short_values, long_keys, long_values)
    )
    with jax.named_scope("long_hidden"):
        sent, hidden_near, match, query, gains, w_query, w_key, keys = call(
            select_kernel,
            (
                wide,
                shape((rows, 128), F32),
                state,
                like(s_qk),
                shape(w_qkv.shape[1:], BF16),
                shape(w_qkv.shape[1:], BF16),
                like(long_keys),
            ),
            (10**6, 3 * 10**6),
            far=(long_rows, hidden, s_qk, w_qkv, long_keys),
            out_far=(shape((parties, longs, model), BF16),),
            scratch=(pltpu.SMEM((longs,), jnp.int32), pltpu.VMEM((parties, longs, model), BF16)),
            copies=7,
        )
        received = lax.all_to_all(
            sent, ("req", "head"), 0, 0, axis_index_groups=mixed_groups(parties)
        )
    with jax.named_scope("short_attention"):
        short_out, short_lse, value, own, values = call(
            short_kernel,
            (state, state, state, state, like(long_values)),
            (10**9, 6 * 10**6),
            far=(cache_lengths, w_qkv, short_keys, short_values, long_values),
            near=(hidden_near, query, gains, w_key),
            scratch=(
                pltpu.SMEM((rows,), jnp.int32),
                pltpu.VMEM(w_qkv.shape[1:], BF16),
                pltpu.VMEM(short_keys.shape, BF16),
                pltpu.VMEM(short_values.shape, BF16),
            ),
            copies=6,
        )
    with jax.named_scope("long_attention"):
        (partial,) = call(
            long_kernel,
            (shape((parties, longs, (width // 128 + 1) * 128), F32),),
            (10**9, 4 * 10**6),
            near=(received, gains, w_query, keys, values),
        )
    with jax.named_scope("long_parts"):
        parts = lax.all_to_all(
            partial, "req", 0, 0, axis_index_groups=[centre_first(parties)]
        )
    with jax.named_scope("project"):
        (projected,) = call(
            project_kernel,
            (wide,),
            (2 * 10**10, 10**6),
            near=(parts, short_out, short_lse, value, own, match, w_out),
        )
    with jax.named_scope("sum_heads"):
        other = exchanged(projected, 1)
        (projected,) = call(add_kernel, (wide,), (10**5, 10**5), near=(projected, other))
        other = exchanged(projected, 3)
    with jax.named_scope("mlp"):
        middle, downward = call(
            mlp_kernel,
            (wide, wide),
            (10**8, 5 * 10**6),
            near=(projected, other, hidden, alpha_attn, w_gate_up, w_down, s_gate, s_up),
        )
    with jax.named_scope("sum_units"):
        other = exchanged(downward, 3)
        (downward,) = call(add_kernel, (wide,), (10**5, 10**5), near=(downward, other))
        other = exchanged(downward, 1)
    with jax.named_scope("final"):
        (updated,) = call(
            final_kernel, (wide,), (10**6, 10**5), near=(downward, other, middle, alpha_mlp)
        )
        return updated


def solution(mesh):
    return jax.shard_map(
        on_device,
        mesh=mesh,
        in_specs=(
            P("req", None),
            P(None, None, "head"),
            P("head", None),
            P("head"),
            P(),
            P(None, None, "head"),
            P("head", None),
            P("head"),
            P("head"),
            P(),
            P("req", None, "head"),
            P("req", None, "head"),
            P("req"),
            P(None, "req", "head"),
            P(None, "req", "head"),
            P(),
        ),
        out_specs=P("req", None),
        check_vma=False,
    )
```

```python
import math

import jax
import jax.numpy as jnp
from jax import lax
from jax.experimental import pallas as pl
from jax.experimental.pallas import tpu as pltpu
from jax.sharding import PartitionSpec as P

HEAD_DIM = 64
EPS = 1e-06
LOW = -3e38
F32 = jnp.float32
BF16 = jnp.bfloat16
LANES = 8

VMEM = pl.BlockSpec(memory_space=pltpu.VMEM)
HBM = pl.BlockSpec(memory_space=pltpu.HBM)


def dot(left, right):
    return jnp.dot(left, right, preferred_element_type=F32)


def dot_t(left, right):
    return lax.dot_general(left, right, (((1,), (1,)), ((), ())), preferred_element_type=F32)


def head_masks(width):
    lane = lax.broadcasted_iota(jnp.int32, (1, width), 1)
    return [
        (lane >= h * HEAD_DIM) & (lane < (h + 1) * HEAD_DIM) for h in range(width // HEAD_DIM)
    ]


def head_rows(width):
    sub = lax.broadcasted_iota(jnp.int32, (LANES, width), 0)
    lane = lax.broadcasted_iota(jnp.int32, (LANES, width), 1)
    return (lane >= sub * HEAD_DIM) & (lane < (sub + 1) * HEAD_DIM)


def spread_sums(values, masks, function):
    result = jnp.zeros_like(values)
    for mask in masks:
        total = jnp.sum(jnp.where(mask, values, 0.0), axis=-1, keepdims=True)
        result = jnp.where(mask, function(total), result)
    return result


def head_unit(values, gains, masks):
    scale = spread_sums(values * values, masks, lambda total: lax.rsqrt(total + EPS))
    return (values * scale * gains).astype(BF16).astype(F32)


def row_norm(values):
    return values * lax.rsqrt(jnp.mean(values * values, axis=-1, keepdims=True) + EPS)


def gathered(values, diagonal):
    return jnp.sum(jnp.where(diagonal, values, 0.0), axis=0, keepdims=True)


def start_all(pairs, sems):
    copies = [pltpu.make_async_copy(s, d, sems.at[i]) for i, (s, d) in enumerate(pairs)]
    for copy in copies:
        copy.start()
    return copies


def select_kernel(
    longs_hbm,
    hidden_hbm,
    gains_hbm,
    w_hbm,
    keys_hbm,
    sent_hbm,
    hidden_ref,
    match_ref,
    query_ref,
    gains_ref,
    w_query_ref,
    w_key_ref,
    keys_ref,
    longs_ref,
    sent_ref,
    sems,
):
    copies = start_all(
        [
            (longs_hbm, longs_ref),
            (hidden_hbm, hidden_ref),
            (gains_hbm, gains_ref),
            (w_hbm.at[0], w_query_ref),
            (w_hbm.at[1], w_key_ref),
            (keys_hbm, keys_ref),
        ],
        sems,
    )
    parties, longs, _ = sent_ref.shape
    rows = hidden_ref.shape[0]
    offset = lax.axis_index("req") * rows
    sub = lax.broadcasted_iota(jnp.int32, (8, rows), 0)
    lane = lax.broadcasted_iota(jnp.int32, (8, rows), 1) + offset
    here = jnp.zeros((8, rows), jnp.bool_)
    copies[0].wait()
    for index in range(longs):
        here = here | ((sub == index) & (lane == longs_ref[index]))
    copies[1].wait()
    picked = dot(here.astype(F32).astype(BF16), hidden_ref[...])[:longs].astype(BF16)
    for party in range(parties):
        sent_ref[party] = picked
    out = pltpu.make_async_copy(sent_ref, sent_hbm, sems.at[6])
    out.start()
    row = lax.broadcasted_iota(jnp.int32, match_ref.shape, 0) + offset
    column = lax.broadcasted_iota(jnp.int32, match_ref.shape, 1)
    match = jnp.zeros(match_ref.shape, F32)
    for index in range(longs):
        match = jnp.where((row == longs_ref[index]) & (column == index), 1.0, match)
    match_ref[...] = match
    copies[2].wait()
    copies[3].wait()
    query = dot_t(hidden_ref[...], w_query_ref[...])
    query = head_unit(query, gains_ref[...][None, :], head_masks(query.shape[1]))
    query_ref[...] = query * math.sqrt(HEAD_DIM)
    copies[4].wait()
    copies[5].wait()
    out.wait()


def short_kernel(
    lengths_hbm,
    w_hbm,
    keys_hbm,
    values_hbm,
    long_values_hbm,
    hidden_ref,
    query_ref,
    gains_ref,
    w_key_ref,
    out_ref,
    lse_ref,
    value_ref,
    own_ref,
    long_values_ref,
    lengths_ref,
    w_value_ref,
    keys_ref,
    values_ref,
    sems,
):
    rows, width = out_ref.shape
    halves = [pl.ds(0, rows // 2), pl.ds(rows // 2, rows - rows // 2)]
    copies = start_all(
        [
            (lengths_hbm, lengths_ref),
            (keys_hbm.at[halves[0]], keys_ref.at[halves[0]]),
            (keys_hbm.at[halves[1]], keys_ref.at[halves[1]]),
            (w_hbm.at[2], w_value_ref),
            (values_hbm, values_ref),
            (long_values_hbm, long_values_ref),
        ],
        sems,
    )
    @pl.when(lax.axis_index("req") >= 0)
    def _():
        slots = keys_ref.shape[2]
        masks = head_masks(width)
        diagonal = head_rows(width)
        sub = lax.broadcasted_iota(jnp.int32, (2 * LANES, 2 * slots), 0)
        lane = lax.broadcasted_iota(jnp.int32, (2 * LANES, 2 * slots), 1)
        second = sub >= LANES
        first = jnp.where(second, slots, 0)
        hidden = hidden_ref[...]
        query = query_ref[...]
        pairs = [
            jnp.concatenate(
                [jnp.where(diagonal, query[r + i : r + i + 1], 0.0) for i in range(2)], axis=0
            ).astype(BF16)
            for r in range(0, rows, 2)
        ]
        key = head_unit(dot_t(hidden, w_key_ref[...]), gains_ref[...][None, :], masks)
        own_ref[...] = spread_sums(query * key, masks, lambda total: total)
        copies[0].wait()
        weights, scales = [], []
        for p, r in enumerate(range(0, rows, 2)):
            if r in (0, rows // 2):
                copies[1 + (r > 0)].wait()
            scores = dot(pairs[p], jnp.concatenate([keys_ref[r], keys_ref[r + 1]], axis=1))
            last = jnp.where(second, slots + lengths_ref[r + 1], lengths_ref[r])
            valid = (lane >= first) & (lane < last)
            scores = jnp.where(valid, scores, LOW)
            top = jnp.max(scores, axis=-1, keepdims=True)
            weight = jnp.where(valid, jnp.exp(scores - top), 0.0)
            total = jnp.sum(weight, axis=-1, keepdims=True)
            weights.append(weight.astype(BF16))
            scales.append(1.0 / total)
            lse = top + jnp.log(total)
            for i in range(2):
                part = slice(i * LANES, (i + 1) * LANES)
                lse_ref[r + i : r + i + 1, :] = gathered(lse[part], diagonal)
        copies[3].wait()
        value_ref[...] = dot_t(hidden, w_value_ref[...]).astype(BF16).astype(F32)
        copies[4].wait()
        for p, r in enumerate(range(0, rows, 2)):
            summed = dot_t(weights[p], jnp.concatenate([values_ref[r], values_ref[r + 1]], axis=1))
            summed = summed * scales[p]
            for i in range(2):
                part = slice(i * LANES, (i + 1) * LANES)
                out_ref[r + i : r + i + 1, :] = gathered(summed[part], diagonal)
        copies[5].wait()


def long_kernel(
    received_ref,
    gains_ref,
    w_ref,
    keys_ref,
    values_ref,
    sent_ref,
):
    parties, longs, _ = received_ref.shape
    width = w_ref.shape[0]
    hidden = received_ref[0].astype(F32)
    for party in range(1, parties):
        hidden = hidden + received_ref[party].astype(F32)
    query = dot_t(hidden.astype(BF16), w_ref[...])
    query = head_unit(query, gains_ref[...][None, :], head_masks(width)) * math.sqrt(HEAD_DIM)
    diagonal = head_rows(width)
    scores = [
        dot(jnp.where(diagonal, query[i : i + 1], 0.0).astype(BF16), keys_ref[i])
        for i in range(longs)
    ]
    padded = sent_ref.shape[2]
    sub = lax.broadcasted_iota(jnp.int32, (LANES, padded), 0)
    lane = lax.broadcasted_iota(jnp.int32, (LANES, padded), 1)
    heads = width // HEAD_DIM
    own_columns = (lane >= sub * HEAD_DIM) & (lane < (sub + 1) * HEAD_DIM) & (lane < width)
    slots = [(sub < heads) & (lane == width + k * heads + sub) for k in range(3)]
    outs = []
    for i in range(longs):
        top = jnp.max(scores[i], axis=-1, keepdims=True)
        weights = jnp.exp(scores[i] - top)
        total = jnp.sum(weights, axis=-1, keepdims=True)
        summed = dot_t(weights.astype(BF16), values_ref[i]) / total
        summed = jnp.concatenate([summed, jnp.zeros((LANES, padded - width), F32)], axis=1)
        row = jnp.where(own_columns, summed, 0.0)
        left = top + jnp.log(total)
        for slot in slots:
            term = left.astype(BF16).astype(F32)
            row = jnp.where(slot, term, row)
            left = left - term
        outs.append(jnp.sum(row, axis=0, keepdims=True))
    packed = jnp.concatenate(outs, axis=0).astype(BF16)
    for party in range(parties):
        sent_ref[party] = packed


def project_kernel(
    parts_ref, short_ref, short_lse_ref, value_ref, own_ref, match_ref, w_ref, out_ref
):
    parties, longs, padded = parts_ref.shape
    width = short_ref.shape[1]
    masks = head_masks(width)
    last = padded - 128
    first = width - last

    def on_heads(compact):
        result = jnp.zeros((longs, width), F32)
        for h, mask in enumerate(masks):
            result = jnp.where(mask, compact[:, first + h : first + h + 1], result)
        return result

    heads = len(masks)
    parts = [parts_ref[party].astype(F32) for party in range(parties)]
    lses = []
    for part in parts:
        terms = part[:, last:]
        lses.append(
            terms + pltpu.roll(terms, 128 - heads, 1) + pltpu.roll(terms, 128 - 2 * heads, 1)
        )
    top = lses[0]
    for lse in lses[1:]:
        top = jnp.maximum(top, lse)
    weights = [jnp.exp(lse - top) for lse in lses]
    total = weights[0]
    for weight in weights[1:]:
        total = total + weight
    long_out = jnp.zeros((longs, width), F32)
    for party in range(parties):
        long_out = long_out + on_heads(weights[party] / total) * parts[party][:, :width]
    long_lse = on_heads(top + jnp.log(total))
    cached = short_ref[...]
    lse = short_lse_ref[...]
    for index in range(longs):
        here = match_ref[:, index : index + 1] > 0.5
        cached = jnp.where(here, long_out[index : index + 1], cached)
        lse = jnp.where(here, long_lse[index : index + 1], lse)
    own = own_ref[...]
    top = jnp.maximum(lse, own)
    old = jnp.exp(lse - top)
    new = jnp.exp(own - top)
    attended = (old * cached + new * value_ref[...]) / (old + new)
    out_ref[...] = dot(attended.astype(BF16), w_ref[...]).astype(BF16)


def add_kernel(left_ref, right_ref, out_ref):
    out_ref[...] = (left_ref[...].astype(F32) + right_ref[...].astype(F32)).astype(BF16)


def renormed(left_ref, right_ref, base, alpha_ref):
    total = left_ref[...].astype(F32) + right_ref[...].astype(F32)
    alpha = alpha_ref[...][None, :]
    return row_norm(base + alpha * (row_norm(total) - base)).astype(BF16)


def mlp_kernel(
    left_ref,
    right_ref,
    hidden_ref,
    alpha_ref,
    w_gate_up_ref,
    w_down_ref,
    s_gate_ref,
    s_up_ref,
    mid_ref,
    out_ref,
):
    middle = renormed(left_ref, right_ref, hidden_ref[...].astype(F32), alpha_ref)
    mid_ref[...] = middle
    gate = dot(middle, w_gate_up_ref[0]) * s_gate_ref[...][None, :]
    upward = dot(middle, w_gate_up_ref[1]) * s_up_ref[...][None, :]
    gated = (gate / (1.0 + jnp.exp(-gate)) * upward).astype(BF16)
    out_ref[...] = dot(gated, w_down_ref[...]).astype(BF16)


def final_kernel(left_ref, right_ref, mid_ref, alpha_ref, out_ref):
    out_ref[...] = renormed(left_ref, right_ref, mid_ref[...].astype(F32), alpha_ref)


def call(kernel, outs, cost, far=(), near=(), out_far=(), scratch=(), copies=0):
    far = [pltpu.with_memory_space_constraint(a, pltpu.HBM) for a in far]
    return pl.pallas_call(
        kernel,
        in_specs=[HBM] * len(far) + [VMEM] * len(near),
        out_specs=[HBM] * len(out_far) + [VMEM] * len(outs),
        out_shape=[pltpu.HBM(a.shape, a.dtype) for a in out_far] + list(outs),
        scratch_shapes=list(scratch) + [pltpu.SemaphoreType.DMA((copies,))] * (copies > 0),
        cost_estimate=pl.CostEstimate(flops=cost[0], bytes_accessed=cost[1], transcendentals=0),
        compiler_params=pltpu.CompilerParams(vmem_limit_bytes=32 * 1024 * 1024),
    )(*far, *near)


def like(array):
    return jax.ShapeDtypeStruct(array.shape, array.dtype)


def centre_first(parties):
    return sorted(range(parties), key=lambda r: (r != parties // 2, r))


def mixed_groups(parties):
    places = lax.axis_size("head")
    return [
        [r * places + (h ^ ((r // 2) % 2)) for r in centre_first(parties)] for h in range(places)
    ]


def exchanged(value, step):
    places = lax.axis_size("head")
    return lax.ppermute(value, "head", [(i, i ^ step) for i in range(places)])


def on_device(
    hidden,
    w_qkv,
    w_out,
    s_qk,
    alpha_attn,
    w_gate_up,
    w_down,
    s_up,
    s_gate,
    alpha_mlp,
    short_keys,
    short_values,
    cache_lengths,
    long_keys,
    long_values,
    long_rows,
):
    rows, model = hidden.shape
    width = w_qkv.shape[2]
    longs = long_keys.shape[0]
    parties = lax.axis_size("req")
    shape = jax.ShapeDtypeStruct
    state = shape((rows, width), F32)
    wide = shape((rows, model), BF16)
    w_qkv, short_keys, short_values, long_keys, long_values = (
        jnp.swapaxes(a, 1, 2) for a in (w_qkv, short_keys, short_values, long_keys, long_values)
    )
    with jax.named_scope("long_hidden"):
        sent, hidden_near, match, query, gains, w_query, w_key, keys = call(
            select_kernel,
            (
                wide,
                shape((rows, 128), F32),
                state,
                like(s_qk),
                shape(w_qkv.shape[1:], BF16),
                shape(w_qkv.shape[1:], BF16),
                like(long_keys),
            ),
            (10**6, 3 * 10**6),
            far=(long_rows, hidden, s_qk, w_qkv, long_keys),
            out_far=(shape((parties, longs, model), BF16),),
            scratch=(pltpu.SMEM((longs,), jnp.int32), pltpu.VMEM((parties, longs, model), BF16)),
            copies=7,
        )
        received = lax.all_to_all(
            sent, ("req", "head"), 0, 0, axis_index_groups=mixed_groups(parties)
        )
    with jax.named_scope("short_attention"):
        short_out, short_lse, value, own, values = call(
            short_kernel,
            (state, state, state, state, like(long_values)),
            (10**9, 6 * 10**6),
            far=(cache_lengths, w_qkv, short_keys, short_values, long_values),
            near=(hidden_near, query, gains, w_key),
            scratch=(
                pltpu.SMEM((rows,), jnp.int32),
                pltpu.VMEM(w_qkv.shape[1:], BF16),
                pltpu.VMEM(short_keys.shape, BF16),
                pltpu.VMEM(short_values.shape, BF16),
            ),
            copies=6,
        )
    with jax.named_scope("long_attention"):
        (partial,) = call(
            long_kernel,
            (shape((parties, longs, (width // 128 + 1) * 128), BF16),),
            (10**9, 4 * 10**6),
            near=(received, gains, w_query, keys, values),
        )
    with jax.named_scope("long_parts"):
        parts = lax.all_to_all(
            partial, "req", 0, 0, axis_index_groups=[centre_first(parties)]
        )
    with jax.named_scope("project"):
        (projected,) = call(
            project_kernel,
            (wide,),
            (2 * 10**10, 10**6),
            near=(parts, short_out, short_lse, value, own, match, w_out),
        )
    with jax.named_scope("sum_heads"):
        other = exchanged(projected, 1)
        (projected,) = call(add_kernel, (wide,), (10**5, 10**5), near=(projected, other))
        other = exchanged(projected, 3)
    with jax.named_scope("mlp"):
        middle, downward = call(
            mlp_kernel,
            (wide, wide),
            (10**8, 5 * 10**6),
            near=(projected, other, hidden, alpha_attn, w_gate_up, w_down, s_gate, s_up),
        )
    with jax.named_scope("sum_units"):
        other = exchanged(downward, 3)
        (downward,) = call(add_kernel, (wide,), (10**5, 10**5), near=(downward, other))
        other = exchanged(downward, 1)
    with jax.named_scope("final"):
        (updated,) = call(
            final_kernel, (wide,), (10**6, 10**5), near=(downward, other, middle, alpha_mlp)
        )
        return updated


def solution(mesh):
    return jax.shard_map(
        on_device,
        mesh=mesh,
        in_specs=(
            P("req", None),
            P(None, None, "head"),
            P("head", None),
            P("head"),
            P(),
            P(None, None, "head"),
            P("head", None),
            P("head"),
            P("head"),
            P(),
            P("req", None, "head"),
            P("req", None, "head"),
            P("req"),
            P(None, "req", "head"),
            P(None, "req", "head"),
            P(),
        ),
        out_specs=P("req", None),
        check_vma=False,
    )
```

```python
import math

import jax
import jax.numpy as jnp
from jax import lax
from jax.experimental import pallas as pl
from jax.experimental.pallas import tpu as pltpu
from jax.sharding import PartitionSpec as P

HEAD_DIM = 64
EPS = 1e-06
LOW = -3e38
F32 = jnp.float32
BF16 = jnp.bfloat16
LANES = 8

VMEM = pl.BlockSpec(memory_space=pltpu.VMEM)
HBM = pl.BlockSpec(memory_space=pltpu.HBM)


def dot(left, right):
    return jnp.dot(left, right, preferred_element_type=F32)


def dot_t(left, right):
    return lax.dot_general(left, right, (((1,), (1,)), ((), ())), preferred_element_type=F32)


def head_masks(width):
    lane = lax.broadcasted_iota(jnp.int32, (1, width), 1)
    return [
        (lane >= h * HEAD_DIM) & (lane < (h + 1) * HEAD_DIM) for h in range(width // HEAD_DIM)
    ]


def head_rows(width):
    sub = lax.broadcasted_iota(jnp.int32, (LANES, width), 0)
    lane = lax.broadcasted_iota(jnp.int32, (LANES, width), 1)
    return (lane >= sub * HEAD_DIM) & (lane < (sub + 1) * HEAD_DIM)


def spread_sums(values, masks, function):
    result = jnp.zeros_like(values)
    for mask in masks:
        total = jnp.sum(jnp.where(mask, values, 0.0), axis=-1, keepdims=True)
        result = jnp.where(mask, function(total), result)
    return result


def head_unit(values, gains, masks):
    scale = spread_sums(values * values, masks, lambda total: lax.rsqrt(total + EPS))
    return (values * scale * gains).astype(BF16).astype(F32)


def row_norm(values):
    return values * lax.rsqrt(jnp.mean(values * values, axis=-1, keepdims=True) + EPS)


def gathered(values, diagonal):
    return jnp.sum(jnp.where(diagonal, values, 0.0), axis=0, keepdims=True)


def start_all(pairs, sems):
    copies = [pltpu.make_async_copy(s, d, sems.at[i]) for i, (s, d) in enumerate(pairs)]
    for copy in copies:
        copy.start()
    return copies


def select_kernel(
    longs_hbm,
    hidden_hbm,
    gains_hbm,
    w_hbm,
    keys_hbm,
    sent_hbm,
    hidden_ref,
    match_ref,
    query_ref,
    gains_ref,
    w_query_ref,
    w_key_ref,
    keys_ref,
    longs_ref,
    sent_ref,
    sems,
):
    copies = start_all(
        [
            (longs_hbm, longs_ref),
            (hidden_hbm, hidden_ref),
            (gains_hbm, gains_ref),
            (w_hbm.at[0], w_query_ref),
            (w_hbm.at[1], w_key_ref),
            (keys_hbm, keys_ref),
        ],
        sems,
    )
    parties, longs, _ = sent_ref.shape
    rows = hidden_ref.shape[0]
    offset = lax.axis_index("req") * rows
    sub = lax.broadcasted_iota(jnp.int32, (8, rows), 0)
    lane = lax.broadcasted_iota(jnp.int32, (8, rows), 1) + offset
    here = jnp.zeros((8, rows), jnp.bool_)
    copies[0].wait()
    for index in range(longs):
        here = here | ((sub == index) & (lane == longs_ref[index]))
    copies[1].wait()
    picked = dot(here.astype(F32).astype(BF16), hidden_ref[...])[:longs].astype(BF16)
    for party in range(parties):
        sent_ref[party] = picked
    out = pltpu.make_async_copy(sent_ref, sent_hbm, sems.at[6])
    out.start()
    row = lax.broadcasted_iota(jnp.int32, match_ref.shape, 0) + offset
    column = lax.broadcasted_iota(jnp.int32, match_ref.shape, 1)
    match = jnp.zeros(match_ref.shape, F32)
    for index in range(longs):
        match = jnp.where((row == longs_ref[index]) & (column == index), 1.0, match)
    match_ref[...] = match
    copies[2].wait()
    copies[3].wait()
    query = dot_t(hidden_ref[...], w_query_ref[...])
    query = head_unit(query, gains_ref[...][None, :], head_masks(query.shape[1]))
    query_ref[...] = query * math.sqrt(HEAD_DIM)
    copies[4].wait()
    copies[5].wait()
    out.wait()


def short_kernel(
    lengths_hbm,
    w_hbm,
    keys_hbm,
    values_hbm,
    long_values_hbm,
    hidden_ref,
    query_ref,
    gains_ref,
    w_key_ref,
    out_ref,
    lse_ref,
    value_ref,
    own_ref,
    long_values_ref,
    lengths_ref,
    w_value_ref,
    keys_ref,
    values_ref,
    sems,
):
    rows, width = out_ref.shape
    halves = [pl.ds(0, rows // 2), pl.ds(rows // 2, rows - rows // 2)]
    copies = start_all(
        [
            (lengths_hbm, lengths_ref),
            (keys_hbm.at[halves[0]], keys_ref.at[halves[0]]),
            (keys_hbm.at[halves[1]], keys_ref.at[halves[1]]),
            (w_hbm.at[2], w_value_ref),
            (values_hbm, values_ref),
            (long_values_hbm, long_values_ref),
        ],
        sems,
    )
    @pl.when(lax.axis_index("req") >= 0)
    def _():
        slots = keys_ref.shape[2]
        masks = head_masks(width)
        diagonal = head_rows(width)
        sub = lax.broadcasted_iota(jnp.int32, (2 * LANES, 2 * slots), 0)
        lane = lax.broadcasted_iota(jnp.int32, (2 * LANES, 2 * slots), 1)
        second = sub >= LANES
        first = jnp.where(second, slots, 0)
        hidden = hidden_ref[...]
        query = query_ref[...]
        pairs = [
            jnp.concatenate(
                [jnp.where(diagonal, query[r + i : r + i + 1], 0.0) for i in range(2)], axis=0
            ).astype(BF16)
            for r in range(0, rows, 2)
        ]
        key = head_unit(dot_t(hidden, w_key_ref[...]), gains_ref[...][None, :], masks)
        own_ref[...] = spread_sums(query * key, masks, lambda total: total)
        copies[0].wait()
        weights, scales = [], []
        for p, r in enumerate(range(0, rows, 2)):
            if r in (0, rows // 2):
                copies[1 + (r > 0)].wait()
            scores = dot(pairs[p], jnp.concatenate([keys_ref[r], keys_ref[r + 1]], axis=1))
            last = jnp.where(second, slots + lengths_ref[r + 1], lengths_ref[r])
            valid = (lane >= first) & (lane < last)
            scores = jnp.where(valid, scores, LOW)
            top = jnp.max(scores, axis=-1, keepdims=True)
            weight = jnp.where(valid, jnp.exp(scores - top), 0.0)
            total = jnp.sum(weight, axis=-1, keepdims=True)
            weights.append(weight.astype(BF16))
            scales.append(1.0 / total)
            lse = top + jnp.log(total)
            for i in range(2):
                part = slice(i * LANES, (i + 1) * LANES)
                lse_ref[r + i : r + i + 1, :] = gathered(lse[part], diagonal)
        copies[3].wait()
        value_ref[...] = dot_t(hidden, w_value_ref[...]).astype(BF16).astype(F32)
        copies[4].wait()
        for p, r in enumerate(range(0, rows, 2)):
            summed = dot_t(weights[p], jnp.concatenate([values_ref[r], values_ref[r + 1]], axis=1))
            summed = summed * scales[p]
            for i in range(2):
                part = slice(i * LANES, (i + 1) * LANES)
                out_ref[r + i : r + i + 1, :] = gathered(summed[part], diagonal)
        copies[5].wait()


def long_kernel(
    received_ref,
    gains_ref,
    w_ref,
    keys_ref,
    values_ref,
    sent_ref,
):
    parties, longs, _ = received_ref.shape
    width = w_ref.shape[0]
    hidden = received_ref[0].astype(F32)
    for party in range(1, parties):
        hidden = hidden + received_ref[party].astype(F32)
    query = dot_t(hidden.astype(BF16), w_ref[...])
    query = head_unit(query, gains_ref[...][None, :], head_masks(width)) * math.sqrt(HEAD_DIM)
    diagonal = head_rows(width)
    scores = [
        dot(jnp.where(diagonal, query[i : i + 1], 0.0).astype(BF16), keys_ref[i])
        for i in range(longs)
    ]
    padded = sent_ref.shape[2]
    sub = lax.broadcasted_iota(jnp.int32, (LANES, padded), 0)
    lane = lax.broadcasted_iota(jnp.int32, (LANES, padded), 1)
    kept = ((lane >= sub * HEAD_DIM) & (lane < (sub + 1) * HEAD_DIM) & (lane < width)) | (
        lane == width + sub
    )
    outs = []
    for i in range(longs):
        top = jnp.max(scores[i], axis=-1, keepdims=True)
        weights = jnp.exp(scores[i] - top)
        total = jnp.sum(weights, axis=-1, keepdims=True)
        summed = dot_t(weights.astype(BF16), values_ref[i]) / total
        summed = jnp.concatenate([summed, jnp.zeros((LANES, padded - width), F32)], axis=1)
        row = jnp.where(lane < width, summed, top + jnp.log(total))
        outs.append(jnp.sum(jnp.where(kept, row, 0.0), axis=0, keepdims=True))
    packed = jnp.concatenate(outs, axis=0)
    for party in range(parties):
        sent_ref[party] = packed


def project_kernel(
    parts_ref, short_ref, short_lse_ref, value_ref, own_ref, match_ref, w_ref, out_ref
):
    parties, longs, padded = parts_ref.shape
    width = short_ref.shape[1]
    masks = head_masks(width)
    last = padded - 128
    first = width - last

    def on_heads(compact):
        result = jnp.zeros((longs, width), F32)
        for h, mask in enumerate(masks):
            result = jnp.where(mask, compact[:, first + h : first + h + 1], result)
        return result

    lses = [parts_ref[party][:, last:] for party in range(parties)]
    top = lses[0]
    for lse in lses[1:]:
        top = jnp.maximum(top, lse)
    weights = [jnp.exp(lse - top) for lse in lses]
    total = weights[0]
    for weight in weights[1:]:
        total = total + weight
    long_out = jnp.zeros((longs, width), F32)
    for party in range(parties):
        long_out = long_out + on_heads(weights[party] / total) * parts_ref[party][:, :width]
    long_lse = on_heads(top + jnp.log(total))
    cached = short_ref[...]
    lse = short_lse_ref[...]
    for index in range(longs):
        here = match_ref[:, index : index + 1] > 0.5
        cached = jnp.where(here, long_out[index : index + 1], cached)
        lse = jnp.where(here, long_lse[index : index + 1], lse)
    own = own_ref[...]
    top = jnp.maximum(lse, own)
    old = jnp.exp(lse - top)
    new = jnp.exp(own - top)
    attended = (old * cached + new * value_ref[...]) / (old + new)
    out_ref[...] = dot(attended.astype(BF16), w_ref[...]).astype(BF16)


def add_kernel(left_ref, right_ref, out_ref):
    out_ref[...] = (left_ref[...].astype(F32) + right_ref[...].astype(F32)).astype(BF16)


def renormed(left_ref, right_ref, base, alpha_ref):
    total = left_ref[...].astype(F32) + right_ref[...].astype(F32)
    alpha = alpha_ref[...][None, :]
    return row_norm(base + alpha * (row_norm(total) - base)).astype(BF16)


def mlp_kernel(
    left_ref,
    right_ref,
    hidden_ref,
    alpha_ref,
    w_gate_up_ref,
    w_down_ref,
    s_gate_ref,
    s_up_ref,
    mid_ref,
    out_ref,
):
    middle = renormed(left_ref, right_ref, hidden_ref[...].astype(F32), alpha_ref)
    mid_ref[...] = middle
    gate = dot(middle, w_gate_up_ref[0]) * s_gate_ref[...][None, :]
    upward = dot(middle, w_gate_up_ref[1]) * s_up_ref[...][None, :]
    gated = (gate / (1.0 + jnp.exp(-gate)) * upward).astype(BF16)
    out_ref[...] = dot(gated, w_down_ref[...]).astype(BF16)


def final_kernel(left_ref, right_ref, mid_ref, alpha_ref, out_ref):
    out_ref[...] = renormed(left_ref, right_ref, mid_ref[...].astype(F32), alpha_ref)


def call(kernel, outs, cost, far=(), near=(), out_far=(), scratch=(), copies=0):
    far = [pltpu.with_memory_space_constraint(a, pltpu.HBM) for a in far]
    return pl.pallas_call(
        kernel,
        in_specs=[HBM] * len(far) + [VMEM] * len(near),
        out_specs=[HBM] * len(out_far) + [VMEM] * len(outs),
        out_shape=[pltpu.HBM(a.shape, a.dtype) for a in out_far] + list(outs),
        scratch_shapes=list(scratch) + [pltpu.SemaphoreType.DMA((copies,))] * (copies > 0),
        cost_estimate=pl.CostEstimate(flops=cost[0], bytes_accessed=cost[1], transcendentals=0),
        compiler_params=pltpu.CompilerParams(vmem_limit_bytes=32 * 1024 * 1024),
    )(*far, *near)


def like(array):
    return jax.ShapeDtypeStruct(array.shape, array.dtype)


def centre_first(parties):
    middle = parties // 2
    return sorted(range(parties), key=lambda r: (r != middle, -abs(r // 2 - middle // 2), r))


def mixed_groups(parties):
    places = lax.axis_size("head")
    return [
        [r * places + (h ^ ((r // 2) % 2)) for r in centre_first(parties)] for h in range(places)
    ]


def exchanged(value, step):
    places = lax.axis_size("head")
    return lax.ppermute(value, "head", [(i, i ^ step) for i in range(places)])


def on_device(
    hidden,
    w_qkv,
    w_out,
    s_qk,
    alpha_attn,
    w_gate_up,
    w_down,
    s_up,
    s_gate,
    alpha_mlp,
    short_keys,
    short_values,
    cache_lengths,
    long_keys,
    long_values,
    long_rows,
):
    rows, model = hidden.shape
    width = w_qkv.shape[2]
    longs = long_keys.shape[0]
    parties = lax.axis_size("req")
    shape = jax.ShapeDtypeStruct
    state = shape((rows, width), F32)
    wide = shape((rows, model), BF16)
    w_qkv, short_keys, short_values, long_keys, long_values = (
        jnp.swapaxes(a, 1, 2) for a in (w_qkv, short_keys, short_values, long_keys, long_values)
    )
    with jax.named_scope("long_hidden"):
        sent, hidden_near, match, query, gains, w_query, w_key, keys = call(
            select_kernel,
            (
                wide,
                shape((rows, 128), F32),
                state,
                like(s_qk),
                shape(w_qkv.shape[1:], BF16),
                shape(w_qkv.shape[1:], BF16),
                like(long_keys),
            ),
            (10**6, 3 * 10**6),
            far=(long_rows, hidden, s_qk, w_qkv, long_keys),
            out_far=(shape((parties, longs, model), BF16),),
            scratch=(pltpu.SMEM((longs,), jnp.int32), pltpu.VMEM((parties, longs, model), BF16)),
            copies=7,
        )
        received = lax.all_to_all(
            sent, ("req", "head"), 0, 0, axis_index_groups=mixed_groups(parties)
        )
    with jax.named_scope("short_attention"):
        short_out, short_lse, value, own, values = call(
            short_kernel,
            (state, state, state, state, like(long_values)),
            (10**9, 6 * 10**6),
            far=(cache_lengths, w_qkv, short_keys, short_values, long_values),
            near=(hidden_near, query, gains, w_key),
            scratch=(
                pltpu.SMEM((rows,), jnp.int32),
                pltpu.VMEM(w_qkv.shape[1:], BF16),
                pltpu.VMEM(short_keys.shape, BF16),
                pltpu.VMEM(short_values.shape, BF16),
            ),
            copies=6,
        )
    with jax.named_scope("long_attention"):
        (partial,) = call(
            long_kernel,
            (shape((parties, longs, (width // 128 + 1) * 128), F32),),
            (10**9, 4 * 10**6),
            near=(received, gains, w_query, keys, values),
        )
    with jax.named_scope("long_parts"):
        parts = lax.all_to_all(
            partial, "req", 0, 0, axis_index_groups=[centre_first(parties)]
        )
    with jax.named_scope("project"):
        (projected,) = call(
            project_kernel,
            (wide,),
            (2 * 10**10, 10**6),
            near=(parts, short_out, short_lse, value, own, match, w_out),
        )
    with jax.named_scope("sum_heads"):
        other = exchanged(projected, 1)
        (projected,) = call(add_kernel, (wide,), (10**5, 10**5), near=(projected, other))
        other = exchanged(projected, 3)
    with jax.named_scope("mlp"):
        middle, downward = call(
            mlp_kernel,
            (wide, wide),
            (10**8, 5 * 10**6),
            near=(projected, other, hidden, alpha_attn, w_gate_up, w_down, s_gate, s_up),
        )
    with jax.named_scope("sum_units"):
        other = exchanged(downward, 3)
        (downward,) = call(add_kernel, (wide,), (10**5, 10**5), near=(downward, other))
        other = exchanged(downward, 1)
    with jax.named_scope("final"):
        (updated,) = call(
            final_kernel, (wide,), (10**6, 10**5), near=(downward, other, middle, alpha_mlp)
        )
        return updated


def solution(mesh):
    return jax.shard_map(
        on_device,
        mesh=mesh,
        in_specs=(
            P("req", None),
            P(None, None, "head"),
            P("head", None),
            P("head"),
            P(),
            P(None, None, "head"),
            P("head", None),
            P("head"),
            P("head"),
            P(),
            P("req", None, "head"),
            P("req", None, "head"),
            P("req"),
            P(None, "req", "head"),
            P(None, "req", "head"),
            P(),
        ),
        out_specs=P("req", None),
        check_vma=False,
    )
```

```python
import math

import jax
import jax.numpy as jnp
from jax import lax
from jax.experimental import pallas as pl
from jax.experimental.pallas import tpu as pltpu
from jax.sharding import PartitionSpec as P

HEAD_DIM = 64
EPS = 1e-06
LOW = -3e38
F32 = jnp.float32
BF16 = jnp.bfloat16
LANES = 8

VMEM = pl.BlockSpec(memory_space=pltpu.VMEM)
HBM = pl.BlockSpec(memory_space=pltpu.HBM)


def dot(left, right):
    return jnp.dot(left, right, preferred_element_type=F32)


def dot_t(left, right):
    return lax.dot_general(left, right, (((1,), (1,)), ((), ())), preferred_element_type=F32)


def head_masks(width):
    lane = lax.broadcasted_iota(jnp.int32, (1, width), 1)
    return [
        (lane >= h * HEAD_DIM) & (lane < (h + 1) * HEAD_DIM) for h in range(width // HEAD_DIM)
    ]


def head_rows(width):
    sub = lax.broadcasted_iota(jnp.int32, (LANES, width), 0)
    lane = lax.broadcasted_iota(jnp.int32, (LANES, width), 1)
    return (lane >= sub * HEAD_DIM) & (lane < (sub + 1) * HEAD_DIM)


def spread_sums(values, masks, function):
    result = jnp.zeros_like(values)
    for mask in masks:
        total = jnp.sum(jnp.where(mask, values, 0.0), axis=-1, keepdims=True)
        result = jnp.where(mask, function(total), result)
    return result


def head_unit(values, gains, masks):
    scale = spread_sums(values * values, masks, lambda total: lax.rsqrt(total + EPS))
    return (values * scale * gains).astype(BF16).astype(F32)


def row_norm(values):
    return values * lax.rsqrt(jnp.mean(values * values, axis=-1, keepdims=True) + EPS)


def gathered(values, diagonal):
    return jnp.sum(jnp.where(diagonal, values, 0.0), axis=0, keepdims=True)


def start_all(pairs, sems):
    copies = [pltpu.make_async_copy(s, d, sems.at[i]) for i, (s, d) in enumerate(pairs)]
    for copy in copies:
        copy.start()
    return copies


def select_kernel(
    longs_hbm,
    hidden_hbm,
    gains_hbm,
    w_hbm,
    keys_hbm,
    sent_hbm,
    hidden_ref,
    match_ref,
    query_ref,
    gains_ref,
    w_query_ref,
    w_key_ref,
    keys_ref,
    longs_ref,
    sent_ref,
    sems,
):
    copies = start_all(
        [
            (longs_hbm, longs_ref),
            (hidden_hbm, hidden_ref),
            (gains_hbm, gains_ref),
            (w_hbm.at[0], w_query_ref),
            (w_hbm.at[1], w_key_ref),
            (keys_hbm, keys_ref),
        ],
        sems,
    )
    parties, longs, _ = sent_ref.shape
    rows = hidden_ref.shape[0]
    offset = lax.axis_index("req") * rows
    sub = lax.broadcasted_iota(jnp.int32, (8, rows), 0)
    lane = lax.broadcasted_iota(jnp.int32, (8, rows), 1) + offset
    here = jnp.zeros((8, rows), jnp.bool_)
    copies[0].wait()
    for index in range(longs):
        here = here | ((sub == index) & (lane == longs_ref[index]))
    copies[1].wait()
    picked = dot(here.astype(F32).astype(BF16), hidden_ref[...])[:longs].astype(BF16)
    for party in range(parties):
        sent_ref[party] = picked
    out = pltpu.make_async_copy(sent_ref, sent_hbm, sems.at[6])
    out.start()
    row = lax.broadcasted_iota(jnp.int32, match_ref.shape, 0) + offset
    column = lax.broadcasted_iota(jnp.int32, match_ref.shape, 1)
    match = jnp.zeros(match_ref.shape, F32)
    for index in range(longs):
        match = jnp.where((row == longs_ref[index]) & (column == index), 1.0, match)
    match_ref[...] = match
    copies[2].wait()
    copies[3].wait()
    query = dot_t(hidden_ref[...], w_query_ref[...])
    query = head_unit(query, gains_ref[...][None, :], head_masks(query.shape[1]))
    query_ref[...] = query * math.sqrt(HEAD_DIM)
    copies[4].wait()
    copies[5].wait()
    out.wait()


def short_kernel(
    lengths_hbm,
    w_hbm,
    keys_hbm,
    values_hbm,
    long_values_hbm,
    hidden_ref,
    query_ref,
    gains_ref,
    w_key_ref,
    out_ref,
    lse_ref,
    value_ref,
    own_ref,
    long_values_ref,
    lengths_ref,
    w_value_ref,
    keys_ref,
    values_ref,
    sems,
):
    rows, width = out_ref.shape
    halves = [pl.ds(0, rows // 2), pl.ds(rows // 2, rows - rows // 2)]
    copies = start_all(
        [
            (lengths_hbm, lengths_ref),
            (keys_hbm.at[halves[0]], keys_ref.at[halves[0]]),
            (keys_hbm.at[halves[1]], keys_ref.at[halves[1]]),
            (w_hbm.at[2], w_value_ref),
            (values_hbm, values_ref),
            (long_values_hbm, long_values_ref),
        ],
        sems,
    )
    @pl.when(lax.axis_index("req") >= 0)
    def _():
        slots = keys_ref.shape[2]
        masks = head_masks(width)
        diagonal = head_rows(width)
        sub = lax.broadcasted_iota(jnp.int32, (2 * LANES, 2 * slots), 0)
        lane = lax.broadcasted_iota(jnp.int32, (2 * LANES, 2 * slots), 1)
        second = sub >= LANES
        first = jnp.where(second, slots, 0)
        hidden = hidden_ref[...]
        query = query_ref[...]
        pairs = [
            jnp.concatenate(
                [jnp.where(diagonal, query[r + i : r + i + 1], 0.0) for i in range(2)], axis=0
            ).astype(BF16)
            for r in range(0, rows, 2)
        ]
        key = head_unit(dot_t(hidden, w_key_ref[...]), gains_ref[...][None, :], masks)
        own_ref[...] = spread_sums(query * key, masks, lambda total: total)
        copies[0].wait()
        weights, scales = [], []
        for p, r in enumerate(range(0, rows, 2)):
            if r in (0, rows // 2):
                copies[1 + (r > 0)].wait()
            scores = dot(pairs[p], jnp.concatenate([keys_ref[r], keys_ref[r + 1]], axis=1))
            last = jnp.where(second, slots + lengths_ref[r + 1], lengths_ref[r])
            valid = (lane >= first) & (lane < last)
            scores = jnp.where(valid, scores, LOW)
            top = jnp.max(scores, axis=-1, keepdims=True)
            weight = jnp.where(valid, jnp.exp(scores - top), 0.0)
            total = jnp.sum(weight, axis=-1, keepdims=True)
            weights.append(weight.astype(BF16))
            scales.append(1.0 / total)
            lse = top + jnp.log(total)
            for i in range(2):
                part = slice(i * LANES, (i + 1) * LANES)
                lse_ref[r + i : r + i + 1, :] = gathered(lse[part], diagonal)
        copies[3].wait()
        value_ref[...] = dot_t(hidden, w_value_ref[...]).astype(BF16).astype(F32)
        copies[4].wait()
        for p, r in enumerate(range(0, rows, 2)):
            summed = dot_t(weights[p], jnp.concatenate([values_ref[r], values_ref[r + 1]], axis=1))
            summed = summed * scales[p]
            for i in range(2):
                part = slice(i * LANES, (i + 1) * LANES)
                out_ref[r + i : r + i + 1, :] = gathered(summed[part], diagonal)
        copies[5].wait()


def long_kernel(
    received_ref,
    gains_ref,
    w_ref,
    keys_ref,
    values_ref,
    sent_ref,
):
    parties, longs, _ = received_ref.shape
    width = w_ref.shape[0]
    hidden = received_ref[0].astype(F32)
    for party in range(1, parties):
        hidden = hidden + received_ref[party].astype(F32)
    query = dot_t(hidden.astype(BF16), w_ref[...])
    query = head_unit(query, gains_ref[...][None, :], head_masks(width)) * math.sqrt(HEAD_DIM)
    diagonal = head_rows(width)
    scores = [
        dot(jnp.where(diagonal, query[i : i + 1], 0.0).astype(BF16), keys_ref[i])
        for i in range(longs)
    ]
    padded = sent_ref.shape[2]
    sub = lax.broadcasted_iota(jnp.int32, (LANES, padded), 0)
    lane = lax.broadcasted_iota(jnp.int32, (LANES, padded), 1)
    kept = ((lane >= sub * HEAD_DIM) & (lane < (sub + 1) * HEAD_DIM) & (lane < width)) | (
        lane == width + sub
    )
    outs = []
    for i in range(longs):
        top = jnp.max(scores[i], axis=-1, keepdims=True)
        weights = jnp.exp(scores[i] - top)
        total = jnp.sum(weights, axis=-1, keepdims=True)
        summed = dot_t(weights.astype(BF16), values_ref[i]) / total
        summed = jnp.concatenate([summed, jnp.zeros((LANES, padded - width), F32)], axis=1)
        row = jnp.where(lane < width, summed, top + jnp.log(total))
        outs.append(jnp.sum(jnp.where(kept, row, 0.0), axis=0, keepdims=True))
    packed = jnp.concatenate(outs, axis=0)
    for party in range(parties):
        sent_ref[party] = packed


def project_kernel(
    parts_ref, short_ref, short_lse_ref, value_ref, own_ref, match_ref, w_ref, out_ref
):
    parties, longs, padded = parts_ref.shape
    width = short_ref.shape[1]
    masks = head_masks(width)
    last = padded - 128
    first = width - last

    def on_heads(compact):
        result = jnp.zeros((longs, width), F32)
        for h, mask in enumerate(masks):
            result = jnp.where(mask, compact[:, first + h : first + h + 1], result)
        return result

    lses = [parts_ref[party][:, last:] for party in range(parties)]
    top = lses[0]
    for lse in lses[1:]:
        top = jnp.maximum(top, lse)
    weights = [jnp.exp(lse - top) for lse in lses]
    total = weights[0]
    for weight in weights[1:]:
        total = total + weight
    long_out = jnp.zeros((longs, width), F32)
    for party in range(parties):
        long_out = long_out + on_heads(weights[party] / total) * parts_ref[party][:, :width]
    long_lse = on_heads(top + jnp.log(total))
    cached = short_ref[...]
    lse = short_lse_ref[...]
    for index in range(longs):
        here = match_ref[:, index : index + 1] > 0.5
        cached = jnp.where(here, long_out[index : index + 1], cached)
        lse = jnp.where(here, long_lse[index : index + 1], lse)
    own = own_ref[...]
    top = jnp.maximum(lse, own)
    old = jnp.exp(lse - top)
    new = jnp.exp(own - top)
    attended = (old * cached + new * value_ref[...]) / (old + new)
    out_ref[...] = dot(attended.astype(BF16), w_ref[...]).astype(BF16)


def add_kernel(left_ref, right_ref, out_ref):
    out_ref[...] = (left_ref[...].astype(F32) + right_ref[...].astype(F32)).astype(BF16)


def renormed(left_ref, right_ref, base, alpha_ref):
    total = left_ref[...].astype(F32) + right_ref[...].astype(F32)
    alpha = alpha_ref[...][None, :]
    return row_norm(base + alpha * (row_norm(total) - base)).astype(BF16)


def mlp_kernel(
    left_ref,
    right_ref,
    hidden_ref,
    alpha_ref,
    w_gate_up_ref,
    w_down_ref,
    s_gate_ref,
    s_up_ref,
    mid_ref,
    out_ref,
):
    middle = renormed(left_ref, right_ref, hidden_ref[...].astype(F32), alpha_ref)
    mid_ref[...] = middle
    gate = dot(middle, w_gate_up_ref[0]) * s_gate_ref[...][None, :]
    upward = dot(middle, w_gate_up_ref[1]) * s_up_ref[...][None, :]
    gated = (gate / (1.0 + jnp.exp(-gate)) * upward).astype(BF16)
    out_ref[...] = dot(gated, w_down_ref[...]).astype(BF16)


def final_kernel(own_ref, far_ref, near_ref, side_ref, mid_ref, alpha_ref, out_ref):
    here = own_ref[...].astype(F32) + near_ref[...].astype(F32)
    total = here + (far_ref[...].astype(F32) + side_ref[...].astype(F32))
    base = mid_ref[...].astype(F32)
    alpha = alpha_ref[...][None, :]
    out_ref[...] = row_norm(base + alpha * (row_norm(total) - base)).astype(BF16)


def call(kernel, outs, cost, far=(), near=(), out_far=(), scratch=(), copies=0):
    far = [pltpu.with_memory_space_constraint(a, pltpu.HBM) for a in far]
    return pl.pallas_call(
        kernel,
        in_specs=[HBM] * len(far) + [VMEM] * len(near),
        out_specs=[HBM] * len(out_far) + [VMEM] * len(outs),
        out_shape=[pltpu.HBM(a.shape, a.dtype) for a in out_far] + list(outs),
        scratch_shapes=list(scratch) + [pltpu.SemaphoreType.DMA((copies,))] * (copies > 0),
        cost_estimate=pl.CostEstimate(flops=cost[0], bytes_accessed=cost[1], transcendentals=0),
        compiler_params=pltpu.CompilerParams(vmem_limit_bytes=32 * 1024 * 1024),
    )(*far, *near)


def like(array):
    return jax.ShapeDtypeStruct(array.shape, array.dtype)


def centre_first(parties):
    return sorted(range(parties), key=lambda r: (r != parties // 2, r))


def mixed_groups(parties):
    places = lax.axis_size("head")
    return [
        [r * places + (h ^ ((r // 2) % 2)) for r in centre_first(parties)] for h in range(places)
    ]


def exchanged(value, step):
    places = lax.axis_size("head")
    return lax.ppermute(value, "head", [(i, i ^ step) for i in range(places)])


def on_device(
    hidden,
    w_qkv,
    w_out,
    s_qk,
    alpha_attn,
    w_gate_up,
    w_down,
    s_up,
    s_gate,
    alpha_mlp,
    short_keys,
    short_values,
    cache_lengths,
    long_keys,
    long_values,
    long_rows,
):
    rows, model = hidden.shape
    width = w_qkv.shape[2]
    longs = long_keys.shape[0]
    parties = lax.axis_size("req")
    shape = jax.ShapeDtypeStruct
    state = shape((rows, width), F32)
    wide = shape((rows, model), BF16)
    w_qkv, short_keys, short_values, long_keys, long_values = (
        jnp.swapaxes(a, 1, 2) for a in (w_qkv, short_keys, short_values, long_keys, long_values)
    )
    with jax.named_scope("long_hidden"):
        sent, hidden_near, match, query, gains, w_query, w_key, keys = call(
            select_kernel,
            (
                wide,
                shape((rows, 128), F32),
                state,
                like(s_qk),
                shape(w_qkv.shape[1:], BF16),
                shape(w_qkv.shape[1:], BF16),
                like(long_keys),
            ),
            (10**6, 3 * 10**6),
            far=(long_rows, hidden, s_qk, w_qkv, long_keys),
            out_far=(shape((parties, longs, model), BF16),),
            scratch=(pltpu.SMEM((longs,), jnp.int32), pltpu.VMEM((parties, longs, model), BF16)),
            copies=7,
        )
        received = lax.all_to_all(
            sent, ("req", "head"), 0, 0, axis_index_groups=mixed_groups(parties)
        )
    with jax.named_scope("short_attention"):
        short_out, short_lse, value, own, values = call(
            short_kernel,
            (state, state, state, state, like(long_values)),
            (10**9, 6 * 10**6),
            far=(cache_lengths, w_qkv, short_keys, short_values, long_values),
            near=(hidden_near, query, gains, w_key),
            scratch=(
                pltpu.SMEM((rows,), jnp.int32),
                pltpu.VMEM(w_qkv.shape[1:], BF16),
                pltpu.VMEM(short_keys.shape, BF16),
                pltpu.VMEM(short_values.shape, BF16),
            ),
            copies=6,
        )
    with jax.named_scope("long_attention"):
        (partial,) = call(
            long_kernel,
            (shape((parties, longs, (width // 128 + 1) * 128), F32),),
            (10**9, 4 * 10**6),
            near=(received, gains, w_query, keys, values),
        )
    with jax.named_scope("long_parts"):
        parts = lax.all_to_all(
            partial, "req", 0, 0, axis_index_groups=[centre_first(parties)]
        )
    with jax.named_scope("project"):
        (projected,) = call(
            project_kernel,
            (wide,),
            (2 * 10**10, 10**6),
            near=(parts, short_out, short_lse, value, own, match, w_out),
        )
    with jax.named_scope("sum_heads"):
        other = exchanged(projected, 1)
        (projected,) = call(add_kernel, (wide,), (10**5, 10**5), near=(projected, other))
        other = exchanged(projected, 3)
    with jax.named_scope("mlp"):
        middle, downward = call(
            mlp_kernel,
            (wide, wide),
            (10**8, 5 * 10**6),
            near=(projected, other, hidden, alpha_attn, w_gate_up, w_down, s_gate, s_up),
        )
    with jax.named_scope("sum_units"):
        others = [exchanged(downward, step) for step in (3, 1, 2)]
    with jax.named_scope("final"):
        (updated,) = call(
            final_kernel, (wide,), (10**6, 10**5), near=(downward, *others, middle, alpha_mlp)
        )
        return updated


def solution(mesh):
    return jax.shard_map(
        on_device,
        mesh=mesh,
        in_specs=(
            P("req", None),
            P(None, None, "head"),
            P("head", None),
            P("head"),
            P(),
            P(None, None, "head"),
            P("head", None),
            P("head"),
            P("head"),
            P(),
            P("req", None, "head"),
            P("req", None, "head"),
            P("req"),
            P(None, "req", "head"),
            P(None, "req", "head"),
            P(),
        ),
        out_specs=P("req", None),
        check_vma=False,
    )
```
